256 devices in a mesh: ctx: 32 (over x, z), head: 8 (over y, core).
Axes of the slice: x: 4, y: 4, z: 8, core: 2. Of those that a mesh axis runs over, the one named last changes fastest.
Arguments:
- query: bfloat16 [6144, 73728], P('ctx', 'head'), may hold values from -40 to 40
- latent: bfloat16 [6144, 576], P('ctx'), may hold values from -6 to 6
- segment: int32 [6144], P('ctx'), may hold values from 0 to 63, never falling along the last dimension, each value on 1 to 385 neighbouring positions
- d_out: bfloat16 [6144, 65536], P('ctx', 'head'), may hold values from -6 to 6
Outputs:
- attended: bfloat16 [6144, 65536], P('ctx', 'head')
- d_query: bfloat16 [6144, 73728], P('ctx', 'head')
- d_latent: float32 [6144, 576], P('ctx')
The draws below stay inside these ranges and needn't reach their ends.
Inputs may be any that keep to these rules, and one draw needn't show every extreme that they name: `segment`: document ids never fall along the window; every document has 1 to 385 tokens and one has exactly 385.
All inputs are finite; a program needn't handle non-finite values.
Results may differ from the reference program's by a relative error of at most 0.017.
Values may be sent and summed in bfloat16 or wider, within the bound.
A program may use at most 128 MiB of HBM per device.

```python
import math
import jax
import jax.numpy as jnp
import numpy as np
from jax import lax

LATENT = 512
ROPE = 64
TOK_DEV = 192
SPAN = 2
HEADS = 128
TOKENS = 6144
MAXDOC = 385
DOCS = 64
N_CTX = 32


def drawn_rows(key):
    return jnp.clip(jax.random.normal(key, (TOKENS, LATENT + ROPE), jnp.float32), -6.0, 6.0)


def draw_latent(key, part):
    rows = drawn_rows(key)
    return rows.astype(jnp.bfloat16)


def draw_query(key, part):
    key = jax.random.fold_in(key, 5)
    first = jax.random.fold_in(key, 0)
    drawn = jnp.clip(jax.random.normal(first, (TOKENS, HEADS, LATENT + ROPE), jnp.float32), -6.0, 6.0)
    return drawn.reshape(TOKENS, HEADS * (LATENT + ROPE)).astype(jnp.bfloat16)


def block_levels(key, extent, pieces, low, high):
    def one(axis_at, parts):
        steps = jax.random.uniform(jax.random.fold_in(jax.random.fold_in(key, 6), axis_at), (parts,), jnp.float32, low / len(pieces), high / len(pieces))
        return jnp.repeat(jnp.exp(steps), extent[axis_at] // parts).reshape((-1,) + (1,) * (len(extent) - axis_at - 1))

    gain = one(*pieces[0])
    for cut in pieces[1:]:
        gain = gain * one(*cut)
    return gain


def split_up(number_of, total, bound, slope):
    portions = [(1 << 20) // math.isqrt(rank ** slope) + 1 for rank in range(2, number_of + 1)]
    spare, holding = total - bound - (number_of - 1), [1] * (number_of - 1)
    while spare > 0:
        free = [i for i in range(number_of - 1) if holding[i] < bound]
        whole, remaining = sum([portions[i] for i in free]), spare
        for i in free:
            more = min(bound - holding[i], max(1, remaining * portions[i] // whole), spare)
            holding[i] = holding[i] + more
            spare = spare - more
    return np.array([bound] + holding)


def uneven_parts(key, number_of, total, limit, slope):
    if number_of == 2:
        one = jax.random.randint(key, (), max(1, total - limit), min(limit, total - 1) + 1)
        return jnp.stack([one, total - one])
    lengths = jnp.asarray(split_up(number_of, total, limit, slope), jnp.int32)
    couples = (number_of - 1) // 2
    giver, receiver = lengths[1:1 + 2 * couples:2], lengths[2:2 + 2 * couples:2]
    margin = jnp.minimum(giver - 1, limit - receiver)
    shifted = jax.random.randint(jax.random.fold_in(key, 1), (couples,), 0, 1 << 20) % (margin + 1)
    lengths = lengths.at[1:1 + 2 * couples:2].set(giver - shifted).at[2:2 + 2 * couples:2].set(receiver + shifted)
    return lengths[jax.random.permutation(jax.random.fold_in(key, 2), number_of)]


def normal_values(key, extent, deviation, reach, shards=(), kind=jnp.bfloat16):
    level = block_levels(key, extent, shards, -0.22, 0.18) if shards else 1.0
    drawn = jax.random.normal(key, extent, jnp.float32) * deviation * level
    return jnp.minimum(jnp.maximum(drawn, -reach), reach).astype(kind)


def setup_inputs(seed: int = 0) -> dict:
    splits = jax.random.split(jax.random.key(seed), 5)
    query = draw_query(jax.random.fold_in(splits[4], 71), 0)
    latent = draw_latent(jax.random.fold_in(splits[4], 71), 0)
    segment = jnp.searchsorted(jnp.cumsum(uneven_parts(splits[2], DOCS, TOKENS, MAXDOC, 1)), jnp.arange(TOKENS), side="right").astype(jnp.int32)
    d_out = normal_values(splits[3], (TOKENS, HEADS * LATENT), 1.0, 6.0, ((0, 32), (1, 8)))
    return dict(query=query, latent=latent, segment=segment, d_out=d_out)


score_scale = 192.0 ** -0.5


def reference(query, latent, segment, d_out):
    width = LATENT + ROPE
    heads = query.shape[1] // width
    front = SPAN * TOK_DEV
    padded = jnp.concatenate([jnp.zeros((front, width), latent.dtype), latent], 0)
    seg_pad = jnp.concatenate([jnp.full((front,), -1, jnp.int32), segment.astype(jnp.int32)], 0)
    span_rows = (SPAN + 1) * TOK_DEV

    def one_block(index):
        start = (index * TOK_DEV).astype(jnp.int32)
        qblock = lax.dynamic_slice_in_dim(query, start, TOK_DEV, 0).reshape(TOK_DEV, heads, width).astype(jnp.float32)
        dblock = lax.dynamic_slice_in_dim(d_out, start, TOK_DEV, 0).reshape(TOK_DEV, heads, LATENT).astype(jnp.float32)
        keys = lax.dynamic_slice_in_dim(padded, start, span_rows, 0).astype(jnp.float32)
        seg_keys = lax.dynamic_slice_in_dim(seg_pad, start, span_rows, 0)
        seg_query = lax.dynamic_slice_in_dim(seg_pad, start + front, TOK_DEV, 0)
        qpos = jnp.arange(TOK_DEV, dtype=jnp.int32) + front
        kpos = jnp.arange(span_rows, dtype=jnp.int32)
        allowed = (seg_query[:, None] == seg_keys[None, :]) & (kpos[None, :] <= qpos[:, None])
        scores = jnp.einsum('qhd,kd->hqk', qblock, keys) * score_scale
        scores = jnp.where(allowed[None], scores, -1e30)
        top = jnp.max(scores, -1, keepdims=True)
        expo = jnp.where(allowed[None], jnp.exp(scores - top), 0.0)
        prob = expo / jnp.sum(expo, -1, keepdims=True)
        prob_low = prob.astype(jnp.bfloat16).astype(jnp.float32)
        values = keys[:, :LATENT]
        attended = jnp.einsum('hqk,kd->qhd', prob_low, values).astype(jnp.bfloat16)
        d_prob = jnp.einsum('qhd,kd->hqk', dblock, values)
        delta = jnp.einsum('qhd,qhd->hq', dblock, attended.astype(jnp.float32))
        d_score = (score_scale * prob * (d_prob - delta[:, :, None])).astype(jnp.bfloat16).astype(jnp.float32)
        d_query = jnp.einsum('hqk,kd->qhd', d_score, keys).astype(jnp.bfloat16)
        d_keys = jnp.einsum('hqk,qhd->kd', d_score, qblock)
        d_vals = jnp.einsum('hqk,qhd->kd', prob_low, dblock)
        d_keys = d_keys + jnp.pad(d_vals, ((0, 0), (0, ROPE)))
        return attended.reshape(TOK_DEV, heads * LATENT), d_query.reshape(TOK_DEV, heads * width), d_keys

    attended, d_query, d_keys = lax.map(one_block, jnp.arange(N_CTX, dtype=jnp.int32))
    d_keys = d_keys.reshape(N_CTX, SPAN + 1, TOK_DEV, width)
    total = jnp.zeros((N_CTX + SPAN, TOK_DEV, width), jnp.float32)
    for slot in range(SPAN + 1):
        total = total.at[slot:slot + N_CTX].add(d_keys[:, slot])
    d_latent = total[SPAN:].reshape(N_CTX * TOK_DEV, width)
    return attended.reshape(N_CTX * TOK_DEV, heads * LATENT), d_query.reshape(N_CTX * TOK_DEV, heads * width), d_latent
```

```python
import jax
import jax.numpy as jnp
from jax import lax
from jax.experimental import pallas as pl
from jax.experimental.pallas import tpu as pltpu
from jax.sharding import PartitionSpec as P

SPAN = 2
TOK = 192
HEADS = 16
PAIRS = HEADS // 2
LAT = 512
WIDTH = 576
PADW = 640
WIN = 512
NCTX = 32
SLICE = 48
HALF = 24
SCALE = 192.0 ** -0.5
SCALE2 = SCALE * 1.4426950408889634
bf16 = jnp.bfloat16
f32 = jnp.float32

GROUPS = ((0, 0, 128, 2, 4, 0), (64, 128, 64, 4, 2, 8))


def dot(a, b):
    return jnp.dot(a, b, preferred_element_type=f32)


def remote(src, dst, send, recv, ctx, head):
    return pltpu.make_async_remote_copy(
        src_ref=src,
        dst_ref=dst,
        send_sem=send,
        recv_sem=recv,
        device_id={"ctx": ctx, "head": head},
        device_id_type=pl.DeviceIdType.MESH,
    )


def kernel(
    q_hbm, lat_ref, seg_ref, do_hbm,
    att_hbm, dq_hbm, dl_hbm,
    q, do, ke, ko, kte, kto, pst, dst, p, ds, att, dq, bias0, bias1, segs,
    acce, acco, accv, hsum, xs_send, xs_recv, yb_send, yb_recv, zb_send, zb_recv,
    ob_send, ob_recv, tsum, fx_recv, out_v,
    in_sem, out_sem, send_sem, recv_sem,
):
    here = lax.axis_index("ctx")
    head = lax.axis_index("head")
    y = head // 2
    c = lax.rem(head, 2)
    sib = y * 2 + 1 - c

    def peer(d):
        return lax.rem(y + d, 4) * 2 + c

    nxt = lax.rem(here + 1 + c, NCTX)
    prv = lax.rem(here + NCTX - 1 - c, NCTX)

    loads = []
    for i in range(PAIRS):
        loads.append(
            (
                pltpu.make_async_copy(
                    q_hbm.at[:, pl.ds(2 * WIDTH * i, 2 * WIDTH)], q.at[i], in_sem.at[0, i]
                ),
                pltpu.make_async_copy(
                    do_hbm.at[:, pl.ds(2 * LAT * i, 2 * LAT)], do.at[i], in_sem.at[1, i]
                ),
            )
        )
    for pair in loads:
        for cp in pair:
            cp.start()

    barrier = pltpu.get_barrier_semaphore()
    for ctx, hd in ((nxt, head), (prv, head), (here, sib), (here, peer(1)), (here, peer(2)), (here, peer(3))):
        pl.semaphore_signal(
            barrier, inc=1, device_id={"ctx": ctx, "head": hd}, device_id_type=pl.DeviceIdType.MESH
        )
    own = lat_ref[...]
    zcol = jnp.zeros((TOK, PADW - WIDTH), bf16)
    ke[2 * TOK :, :] = jnp.concatenate([own, zcol], 1)
    segs[2] = seg_ref[...]
    pl.semaphore_wait(barrier, 6)

    mine = (1 - c) * TOK
    other = c * TOK

    def rows(base, yy):
        return pl.ds(pl.multiple_of(base + yy * SLICE, 16), SLICE)

    h1 = remote(
        ke.at[rows(2 * TOK, y)], ke.at[rows(mine, y)], send_sem.at[0], recv_sem.at[0], nxt, head
    )
    h1.start()
    s1 = remote(segs.at[2], segs.at[1 - c], send_sem.at[1], recv_sem.at[1], nxt, head)
    s1.start()
    s1.wait_recv()
    s2 = remote(segs.at[1 - c], segs.at[1 - c], send_sem.at[2], recv_sem.at[2], here, sib)
    s2.start()
    h1.wait_recv()
    sends = [h1, s1, s2]
    h2 = []
    for d in (1, 3, 2):
        cp = remote(
            ke.at[rows(mine, y)], ke.at[rows(mine, y)],
            send_sem.at[2 + d], recv_sem.at[2 + d], here, peer(d),
        )
        cp.start()
        h2.append((d, cp))
    sends += [cp for _, cp in h2]
    fwd = [
        remote(
            ke.at[rows(mine, y)], ke.at[rows(mine, y)], send_sem.at[6], recv_sem.at[6], here, sib
        )
    ]
    fwd[0].start()
    for d, cp in h2:
        cp.wait_recv()
        yy = lax.rem(y + 4 - d, 4)
        fw = remote(
            ke.at[rows(mine, yy)], ke.at[rows(mine, yy)],
            send_sem.at[6 + d], recv_sem.at[6 + d], here, sib,
        )
        fw.start()
        fwd.append(fw)
    s2.wait_recv()
    sends += fwd

    seg_row = jnp.concatenate(
        [
            jnp.where(here >= 2, segs[0], -1),
            jnp.where(here >= 1, segs[1], -1),
            segs[2],
        ],
        1,
    )
    seg_keys = jnp.broadcast_to(seg_row, (TOK, 3 * TOK))
    tok = lax.broadcasted_iota(jnp.int32, (TOK, 3 * TOK), 0) + 2 * TOK
    key = lax.broadcasted_iota(jnp.int32, (TOK, 3 * TOK), 1)
    seg_q = jnp.sum(jnp.where(tok == key, seg_keys, 0), 1, keepdims=True)
    bias = jnp.where((seg_q == seg_keys) & (key <= tok), 0.0, -1e30)
    bias0[...] = bias[:128, :WIN]
    bias1[...] = bias[128:, 64:]

    for fw in fwd:
        fw.wait_recv()
    for cp in sends:
        cp.wait_send()

    kev = ke[...]
    zk = jnp.zeros((3 * TOK, PADW - WIDTH), bf16)
    ko[...] = jnp.concatenate([zk, kev[:, :WIDTH]], 1)
    for g in (0, 1):
        st = GROUPS[g][0]
        kt = kev[st : st + WIN].T
        kte[g] = kt
        kto[g] = jnp.concatenate([jnp.zeros((PADW - WIDTH, WIN), bf16), kt[:WIDTH]], 0)

    def qrows(g, i, par):
        _, t0, toks, n, _, _ = GROUPS[g]
        return q[pl.ds(i * n, n), t0 : t0 + toks, par * LAT : par * LAT + PADW].reshape(256, PADW)

    def dorows(g, i, par):
        _, t0, toks, n, _, _ = GROUPS[g]
        return do[pl.ds(i * n, n), t0 : t0 + toks, par * LAT : par * LAT + LAT].reshape(256, LAT)

    def attend(g, i, par):
        _, _, toks, n, _, first = GROUPS[g]
        bias_ref = (bias0, bias1)[g]
        s = dot(qrows(g, i, par), (kte, kto)[par][g])
        dp = dot(dorows(g, i, par), kte[g, :LAT, :])
        t = ((s * SCALE2).reshape(n, toks, WIN) + bias_ref[...][None]).reshape(256, WIN)
        e = jnp.exp2(t - jnp.max(t, 1, keepdims=True))
        pr = e * (1.0 / jnp.sum(e, 1, keepdims=True))
        delta = jnp.sum(pr * dp, 1, keepdims=True)
        d = (pr * (dp - delta) * SCALE).astype(bf16)
        pr = pr.astype(bf16)
        j = first + i * 2 + par
        p[j] = pr
        ds[j] = d
        pst[j] = pr.T
        dst[j] = d.T

    def wait_pair(i):
        pltpu.make_async_copy(
            q_hbm.at[:, pl.ds(0, 2 * WIDTH)], q.at[i], in_sem.at[0, i]
        ).wait()
        pltpu.make_async_copy(
            do_hbm.at[:, pl.ds(0, 2 * LAT)], do.at[i], in_sem.at[1, i]
        ).wait()

    def step0(i, _):
        wait_pair(2 * i)
        wait_pair(2 * i + 1)
        attend(0, i, 0)
        attend(0, i, 1)
        return 0

    def step1(i, _):
        attend(1, i, 0)
        attend(1, i, 1)
        return 0

    lax.fori_loop(0, 4, step0, 0)
    lax.fori_loop(0, 2, step1, 0)

    acce[...] = jnp.zeros_like(acce)
    acco[...] = jnp.zeros_like(acco)
    accv[...] = jnp.zeros_like(accv)

    def key_grads(lo, hi):
        for g in (0, 1):
            st, _, _, _, count, first = GROUPS[g]
            a, b = max(lo, st), min(hi, st + WIN)

            def step(i, _):
                j = first + 2 * i
                w = slice(a - st, b - st)
                acce[a:b] += dot(dst[j, w], qrows(g, i, 0))
                acco[a:b] += dot(dst[j + 1, w], qrows(g, i, 1))
                accv[a:b] += dot(pst[j, w], dorows(g, i, 0)) + dot(pst[j + 1, w], dorows(g, i, 1))
                return 0

            lax.fori_loop(0, count, step, 0)
        tot = acce[lo:hi, :WIDTH] + acco[lo:hi, PADW - WIDTH :]
        hsum[lo:hi, :LAT] = tot[:, :LAT] + accv[lo:hi]
        hsum[lo:hi, LAT:] = tot[:, LAT:]

    key_grads(0, 2 * TOK)
    xs_send[...] = hsum[pl.ds(pl.multiple_of(other, 16), TOK)].astype(bf16)
    r1 = remote(xs_send, xs_recv, send_sem.at[10], recv_sem.at[10], here, sib)
    r1.start()
    key_grads(2 * TOK, 3 * TOK)

    ob_send[...] = hsum[2 * TOK :].astype(bf16)
    r1.wait_recv()
    keep = hsum[pl.ds(pl.multiple_of(mine, 16), TOK)] + xs_recv[...].astype(f32)
    yb_send[...] = keep.astype(bf16)
    hsum[:TOK] = keep
    yb = []
    for d in (1, 3, 2):
        cp = remote(
            yb_send.at[rows(0, lax.rem(y + d, 4))], yb_recv.at[d - 1],
            send_sem.at[10 + d], recv_sem.at[10 + d], here, peer(d),
        )
        cp.start()
        yb.append(cp)
    ob = []
    for d in (1, 3, 2):
        cp = remote(
            ob_send.at[rows(0, lax.rem(y + d, 4))], ob_recv.at[d - 1],
            send_sem.at[13 + d], recv_sem.at[13 + d], here, peer(d),
        )
        cp.start()
        ob.append(cp)

    stores = []

    def outputs(g, i):
        st, t0, toks, n, _, first = GROUPS[g]
        j = first + 2 * i
        for par in (0, 1):
            o = dot(p[j + par], ke[st : st + WIN, :LAT]).astype(bf16).reshape(n, toks, LAT)
            for a in range(n):
                col = (2 * (i * n + a) + par) * LAT
                att[t0 : t0 + toks, col : col + LAT] = o[a]
        qe = dot(ds[j], ke[st : st + WIN])
        qo = dot(ds[j + 1], ko[st : st + WIN])
        full = jnp.concatenate(
            [qe[:, :LAT], qe[:, LAT:] + qo[:, : PADW - LAT], qo[:, PADW - LAT :]], 1
        )
        full = full.astype(bf16).reshape(n, toks, 2 * WIDTH)
        for a in range(n):
            col = (i * n + a) * 2 * WIDTH
            dq[t0 : t0 + toks, col : col + 2 * WIDTH] = full[a]
        at = (pl.ds(t0, toks), pl.ds(i * n * 2 * LAT, n * 2 * LAT))
        qt = (pl.ds(t0, toks), pl.ds(i * n * 2 * WIDTH, n * 2 * WIDTH))
        k = len(stores) // 2
        stores.append(pltpu.make_async_copy(att.at[at], att_hbm.at[at], out_sem.at[0, k]))
        stores.append(pltpu.make_async_copy(dq.at[qt], dq_hbm.at[qt], out_sem.at[1, k]))
        stores[-1].start()
        stores[-2].start()

    outputs(0, 0)
    outputs(0, 1)
    outputs(0, 2)
    for cp in yb:
        cp.wait_recv()
    zb_send[...] = (
        hsum[rows(0, y)]
        + yb_recv[0].astype(f32)
        + yb_recv[1].astype(f32)
        + yb_recv[2].astype(f32)
    ).astype(bf16)
    zc = remote(zb_send, zb_recv, send_sem.at[17], recv_sem.at[17], prv, head)
    zc.start()
    outputs(0, 3)
    outputs(1, 0)
    for cp in ob:
        cp.wait_recv()
    tsum[...] = (
        hsum[rows(2 * TOK, y)]
        + ob_recv[0].astype(f32)
        + ob_recv[1].astype(f32)
        + ob_recv[2].astype(f32)
    )
    outputs(1, 1)
    zc.wait_recv()
    tsum[...] += zb_recv[...].astype(f32)

    def half(cc):
        return pl.ds(pl.multiple_of(cc * HALF, 8), HALF)

    fx = remote(tsum.at[half(1 - c)], fx_recv, send_sem.at[18], recv_sem.at[18], here, sib)
    fx.start()
    fx.wait_recv()

    def place(yy, cc):
        return pl.ds(pl.multiple_of(yy * SLICE + cc * HALF, 8), HALF)

    out_v[place(y, c)] = tsum[half(c)] + fx_recv[...]
    spread = []
    for d in (1, 3, 2):
        cp = remote(
            out_v.at[place(y, c)], out_v.at[place(y, c)],
            send_sem.at[18 + d], recv_sem.at[18 + d], here, peer(d),
        )
        cp.start()
        spread.append((d, cp))
    last = [
        remote(
            out_v.at[place(y, c)], out_v.at[place(y, c)], send_sem.at[22], recv_sem.at[22], here, sib
        )
    ]
    last[0].start()
    for d, cp in spread:
        cp.wait_recv()
        yy = lax.rem(y + 4 - d, 4)
        fw = remote(
            out_v.at[place(yy, c)], out_v.at[place(yy, c)],
            send_sem.at[22 + d], recv_sem.at[22 + d], here, sib,
        )
        fw.start()
        last.append(fw)
    for cp in last:
        cp.wait_recv()
    fin = pltpu.make_async_copy(out_v, dl_hbm, out_sem.at[0, 6])
    fin.start()
    for cp in [r1, zc, fx] + yb + ob + [cp for _, cp in spread] + last:
        cp.wait_send()
    for cp in stores:
        cp.wait()
    fin.wait()


def body(query, latent, segment, d_out):
    anyspec = pl.BlockSpec(memory_space=pl.ANY)
    vspec = pl.BlockSpec(memory_space=pltpu.VMEM)
    V = pltpu.VMEM
    return pl.pallas_call(
        kernel,
        out_shape=(
            jax.ShapeDtypeStruct((TOK, HEADS * LAT), bf16),
            jax.ShapeDtypeStruct((TOK, HEADS * WIDTH), bf16),
            jax.ShapeDtypeStruct((TOK, WIDTH), f32),
        ),
        in_specs=[anyspec, vspec, vspec, anyspec],
        out_specs=(anyspec, anyspec, anyspec),
        scratch_shapes=[
            V((PAIRS, TOK, 2 * WIDTH), bf16),
            V((PAIRS, TOK, 2 * LAT), bf16),
            V((3 * TOK, PADW), bf16),
            V((3 * TOK, PADW), bf16),
            V((2, PADW, WIN), bf16),
            V((2, PADW, WIN), bf16),
            V((12, WIN, 256), bf16),
            V((12, WIN, 256), bf16),
            V((12, 256, WIN), bf16),
            V((12, 256, WIN), bf16),
            V((TOK, HEADS * LAT), bf16),
            V((TOK, HEADS * WIDTH), bf16),
            V((128, WIN), f32),
            V((64, WIN), f32),
            V((3, 1, TOK), jnp.int32),
            V((3 * TOK, PADW), f32),
            V((3 * TOK, PADW), f32),
            V((3 * TOK, LAT), f32),
            V((3 * TOK, WIDTH), f32),
            V((TOK, WIDTH), bf16),
            V((TOK, WIDTH), bf16),
            V((TOK, WIDTH), bf16),
            V((3, SLICE, WIDTH), bf16),
            V((SLICE, WIDTH), bf16),
            V((SLICE, WIDTH), bf16),
            V((TOK, WIDTH), bf16),
            V((3, SLICE, WIDTH), bf16),
            V((SLICE, WIDTH), f32),
            V((HALF, WIDTH), f32),
            V((TOK, WIDTH), f32),
            pltpu.SemaphoreType.DMA((2, PAIRS)),
            pltpu.SemaphoreType.DMA((2, PAIRS)),
            pltpu.SemaphoreType.DMA((26,)),
            pltpu.SemaphoreType.DMA((26,)),
        ],
        compiler_params=pltpu.CompilerParams(
            collective_id=0, has_side_effects=True, vmem_limit_bytes=56 << 20
        ),
    )(query, latent, segment.reshape(1, TOK), d_out)


def solution(mesh):
    in_specs = (P("ctx", "head"), P("ctx", None), P("ctx"), P("ctx", "head"))
    out_specs = (P("ctx", "head"), P("ctx", "head"), P("ctx", None))
    return jax.shard_map(body, mesh=mesh, in_specs=in_specs, out_specs=out_specs, check_vma=False)
```

```python
import jax
import jax.numpy as jnp
from jax import lax
from jax.experimental import pallas as pl
from jax.experimental.pallas import tpu as pltpu
from jax.sharding import PartitionSpec as P

TOK = 192
HEADS = 16
PAIRS = HEADS // 2
LAT = 512
WIDTH = 576
PADW = 640
WIN = 512
NCTX = 32
SLICE = 48
PART = 64
SCALE = 192.0 ** -0.5
SCALE2 = SCALE * 1.4426950408889634
bf16 = jnp.bfloat16
f32 = jnp.float32
MESH = pl.DeviceIdType.MESH

GROUPS = ((0, 0, 128, 2, 4, 0), (64, 128, 64, 4, 2, 8))


def dot(a, b):
    return jnp.dot(a, b, preferred_element_type=f32)


def remote(src, dst, send, recv, ctx, head):
    return pltpu.make_async_remote_copy(
        src_ref=src,
        dst_ref=dst,
        send_sem=send,
        recv_sem=recv,
        device_id={"ctx": ctx, "head": head},
        device_id_type=MESH,
    )


def kernel(
    q_hbm, lat_hbm, seg_hbm, do_hbm,
    att, dq, dl,
    q, do, ke, ko, kte, kto, pst, dst, p, ds, bias0, bias1, segs,
    acc, hsum, xs_send, xs_recv, zb_send, zb_recv, ob_send, ob_recv, tb, lat,
    in_sem, send_sem, recv_sem,
):
    here = lax.axis_index("ctx")
    head = lax.axis_index("head")
    y = head // 2
    c = lax.rem(head, 2)
    sib = y * 2 + 1 - c

    def peer(d):
        return lax.rem(y + d, 4) * 2 + c

    has_next = here + 1 + c < NCTX
    has_prev = here >= 1 + c
    sib_prev = here >= 2 - c
    nxt = jnp.minimum(here + 1 + c, NCTX - 1)
    prv = jnp.maximum(here - 1 - c, 0)

    barrier = pltpu.get_barrier_semaphore()

    def greet(ctx, hd):
        pl.semaphore_signal(barrier, inc=1, device_id={"ctx": ctx, "head": hd}, device_id_type=MESH)

    @pl.when(has_next)
    def _():
        for d in range(4):
            greet(nxt, peer(d))

    @pl.when(has_prev)
    def _():
        for d in range(4):
            greet(prv, peer(d))

    greet(here, sib)
    for d in (1, 2, 3):
        greet(here, peer(d))

    get_lat = pltpu.make_async_copy(lat_hbm, lat, in_sem.at[0, PAIRS])
    get_seg = pltpu.make_async_copy(seg_hbm, segs.at[2], in_sem.at[1, PAIRS])
    get_lat.start()
    get_seg.start()

    mine = (1 - c) * TOK
    other = c * TOK

    def rows(base, size):
        return pl.ds(pl.multiple_of(base, 16), size)

    get_seg.wait()
    get_lat.wait()
    ke[2 * TOK :, :] = jnp.concatenate([lat[...], jnp.zeros((TOK, PADW - WIDTH), bf16)], 1)

    @pl.when(jnp.logical_not(has_prev))
    def _():
        ke[rows(mine, TOK), :] = jnp.zeros((TOK, PADW), bf16)
        segs[1 - c] = jnp.full((1, TOK), -1, jnp.int32)

    @pl.when(jnp.logical_not(sib_prev))
    def _():
        ke[rows(other, TOK), :] = jnp.zeros((TOK, PADW), bf16)
        segs[c] = jnp.full((1, TOK), -1, jnp.int32)

    count = 4 + 4 * has_next.astype(jnp.int32) + 4 * has_prev.astype(jnp.int32)
    pl.semaphore_wait(barrier, count)

    def halo(k):
        return remote(
            ke.at[pl.ds(2 * TOK + PART * k, PART)], ke.at[rows(mine + PART * k, PART)],
            send_sem.at[k], recv_sem.at[k], nxt, head,
        )

    def pass_on(k, base):
        w = rows(base + PART * k, PART)
        return remote(ke.at[w], ke.at[w], send_sem.at[4 + k], recv_sem.at[4 + k], here, sib)

    seg_halo = remote(segs.at[2], segs.at[1 - c], send_sem.at[3], recv_sem.at[3], nxt, head)
    seg_pass = remote(segs.at[1 - c], segs.at[1 - c], send_sem.at[7], recv_sem.at[7], here, sib)

    @pl.when(has_next)
    def _():
        seg_halo.start()
        for k in range(3):
            halo(k).start()

    for i in range(PAIRS):
        pltpu.make_async_copy(
            q_hbm.at[:, pl.ds(2 * WIDTH * i, 2 * WIDTH)], q.at[i], in_sem.at[0, i]
        ).start()
        pltpu.make_async_copy(
            do_hbm.at[:, pl.ds(2 * LAT * i, 2 * LAT)], do.at[i], in_sem.at[1, i]
        ).start()

    @pl.when(has_prev)
    def _():
        seg_halo.wait_recv()
        seg_pass.start()
        for k in range(3):
            halo(k).wait_recv()
            pass_on(k, mine).start()

    @pl.when(sib_prev)
    def _():
        seg_pass.wait_recv()

    seg_keys = jnp.broadcast_to(jnp.concatenate([segs[0], segs[1], segs[2]], 1), (TOK, 3 * TOK))
    tok = lax.broadcasted_iota(jnp.int32, (TOK, 3 * TOK), 0) + 2 * TOK
    key = lax.broadcasted_iota(jnp.int32, (TOK, 3 * TOK), 1)
    seg_q = jnp.sum(jnp.where(tok == key, seg_keys, 0), 1, keepdims=True)
    bias = jnp.where((seg_q == seg_keys) & (key <= tok), 0.0, -1e30)
    bias0[...] = bias[:128, :WIN]
    bias1[...] = bias[128:, 64:]

    @pl.when(sib_prev)
    def _():
        for k in range(3):
            pass_on(k, other).wait_recv()

    kev = ke[...]
    ko[...] = jnp.concatenate([jnp.zeros((3 * TOK, PADW - WIDTH), bf16), kev[:, :WIDTH]], 1)
    for g in (0, 1):
        st = GROUPS[g][0]
        kt = kev[st : st + WIN].T
        kte[g] = kt
        kto[g] = jnp.concatenate([jnp.zeros((PADW - WIDTH, WIN), bf16), kt[:WIDTH]], 0)

    def attend(g, i, par):
        _, t0, toks, n, _, first = GROUPS[g]
        bias_ref = (bias0, bias1)[g]
        qs = q[pl.ds(i * n, n), t0 : t0 + toks, par * LAT : par * LAT + PADW].reshape(256, PADW)
        os = do[pl.ds(i * n, n), t0 : t0 + toks, par * LAT : par * LAT + LAT].reshape(256, LAT)
        s = dot(qs, (kte, kto)[par][g])
        dp = dot(os, kte[g, :LAT, :])
        t = ((s * SCALE2).reshape(n, toks, WIN) + bias_ref[...][None]).reshape(256, WIN)
        e = jnp.exp2(t - jnp.max(t, 1, keepdims=True))
        pr = e * (1.0 / jnp.sum(e, 1, keepdims=True))
        delta = jnp.sum(pr * dp, 1, keepdims=True)
        d = (pr * (dp - delta) * SCALE).astype(bf16)
        pr = pr.astype(bf16)
        j = first + i * 2 + par
        p[j] = pr
        ds[j] = d
        cols = pl.ds(pl.multiple_of(g * 1024 + i * 256, 256), 256)
        pst[par, :, cols] = pr.T
        dst[par, :, cols] = d.T

    def wait_pair(i):
        pltpu.make_async_copy(
            q_hbm.at[:, pl.ds(0, 2 * WIDTH)], q.at[i], in_sem.at[0, i]
        ).wait()
        pltpu.make_async_copy(
            do_hbm.at[:, pl.ds(0, 2 * LAT)], do.at[i], in_sem.at[1, i]
        ).wait()

    for i in range(PAIRS):
        wait_pair(i)

    def step0(i, _):
        attend(0, i, 0)
        attend(0, i, 1)
        return 0

    def step1(i, _):
        attend(1, i, 0)
        attend(1, i, 1)
        return 0

    lax.fori_loop(0, 4, step0, 0, unroll=4)
    lax.fori_loop(0, 2, step1, 0, unroll=2)

    def key_grads(lo, hi):
        spans = ((0, lo, min(hi, WIN)), (1, max(lo, 64), hi))
        if hi > WIN:
            spans = spans[::-1]
        for at, (g, a, b) in enumerate(spans):
            st, t0, toks, _, _, _ = GROUPS[g]
            lanes = slice(g * 1024, g * 1024 + toks * PAIRS)
            w = slice(a - st, b - st)
            for par in (0, 1):
                qs = q[:, t0 : t0 + toks, par * LAT : par * LAT + PADW].reshape(toks * PAIRS, PADW)
                r = dot(dst[par, w, lanes], qs)
                acc[par, a:b] = r if at == 0 else acc[par, a:b] + r
            dv = sum(
                dot(
                    pst[par, w, lanes],
                    do[:, t0 : t0 + toks, par * LAT : par * LAT + LAT].reshape(toks * PAIRS, LAT),
                )
                for par in (0, 1)
            )
            acc[0, a:b, :LAT] += dv
        hsum[lo:hi] = acc[0, lo:hi, :WIDTH] + acc[1, lo:hi, PADW - WIDTH :]

    pair_sum = remote(xs_send, xs_recv, send_sem.at[8], recv_sem.at[8], here, sib)

    def send_owners():
        zb_send[...] = (hsum[rows(mine, TOK)] + xs_recv[...].astype(f32)).astype(bf16)

        @pl.when(has_prev)
        def _():
            for d in range(4):
                owner_copy(d).start()

    def owner_copy(d):
        yy = lax.rem(y + d, 4)
        return remote(
            zb_send.at[rows(yy * SLICE, SLICE)], zb_recv.at[y],
            send_sem.at[9 + d], recv_sem.at[9 + y], prv, peer(d),
        )

    def owner_recv(d):
        return remote(
            zb_send.at[pl.ds(0, SLICE)], zb_recv.at[d], send_sem.at[9], recv_sem.at[9 + d], prv, head
        )

    key_grads(0, TOK)

    @pl.when(c == 0)
    def _():
        xs_send[...] = hsum[:TOK].astype(bf16)
        pair_sum.start()

    key_grads(TOK, 2 * TOK)

    @pl.when(c == 1)
    def _():
        xs_send[...] = hsum[TOK : 2 * TOK].astype(bf16)
        pair_sum.start()
        pair_sum.wait_recv()
        send_owners()

    key_grads(2 * TOK, 3 * TOK)
    ob_send[...] = hsum[2 * TOK :].astype(bf16)

    @pl.when(c == 0)
    def _():
        pair_sum.wait_recv()
        send_owners()

    ob = []
    for d in (1, 3, 2):
        cp = remote(
            ob_send.at[rows(lax.rem(y + d, 4) * SLICE, SLICE)], ob_recv.at[d - 1],
            send_sem.at[12 + d], recv_sem.at[12 + d], here, peer(d),
        )
        cp.start()
        ob.append(cp)

    def outputs(g, i):
        st, t0, toks, n, _, first = GROUPS[g]
        j = first + 2 * i
        for par in (0, 1):
            o = dot(p[j + par], ke[st : st + WIN, :LAT]).astype(bf16).reshape(n, toks, LAT)
            for a in range(n):
                col = (2 * (i * n + a) + par) * LAT
                att[t0 : t0 + toks, col : col + LAT] = o[a]
        qe = dot(ds[j], ke[st : st + WIN])
        qo = dot(ds[j + 1], ko[st : st + WIN])
        full = jnp.concatenate(
            [qe[:, :LAT], qe[:, LAT:] + qo[:, : PADW - LAT], qo[:, PADW - LAT :]], 1
        )
        full = full.astype(bf16).reshape(n, toks, 2 * WIDTH)
        for a in range(n):
            col = (i * n + a) * 2 * WIDTH
            dq[t0 : t0 + toks, col : col + 2 * WIDTH] = full[a]

    for i in range(4):
        outputs(0, i)
    for i in range(2):
        outputs(1, i)

    for cp in ob:
        cp.wait_recv()
    part = hsum[pl.ds(pl.multiple_of(2 * TOK + y * SLICE, 8), SLICE)]
    for d in range(3):
        part = part + ob_recv[d].astype(f32)
    hsum[:SLICE] = part

    @pl.when(has_next)
    def _():
        for d in range(4):
            owner_recv(d).wait_recv()
        got = zb_recv[0].astype(f32)
        for d in (1, 2, 3):
            got = got + zb_recv[d].astype(f32)
        hsum[:SLICE] += got

    tb[c, rows(y * SLICE, SLICE)] = hsum[:SLICE].astype(bf16)

    def share(yy, to, k):
        w = (c, rows(yy * SLICE, SLICE))
        return remote(tb.at[w], tb.at[w], send_sem.at[k], recv_sem.at[k], here, to)

    spread = []
    for d in (1, 3, 2):
        cp = share(y, peer(d), 15 + d)
        cp.start()
        spread.append((d, cp))
    last = [share(y, sib, 19)]
    last[0].start()
    for d, cp in spread:
        cp.wait_recv()
        fw = share(lax.rem(y + 4 - d, 4), sib, 19 + d)
        fw.start()
        last.append(fw)
    for cp in last:
        cp.wait_recv()
    dl[...] = tb[0].astype(f32) + tb[1].astype(f32)

    @pl.when(has_next)
    def _():
        seg_halo.wait_send()
        for k in range(3):
            halo(k).wait_send()

    @pl.when(has_prev)
    def _():
        seg_pass.wait_send()
        for k in range(3):
            pass_on(k, mine).wait_send()
        for d in range(4):
            owner_copy(d).wait_send()

    pair_sum.wait_send()
    for cp in ob + [cp for _, cp in spread] + last:
        cp.wait_send()


def write_out(att, dq, dl, att_hbm, dq_hbm, dl_hbm, sem):
    copies = [pltpu.make_async_copy(dl, dl_hbm, sem.at[0])]
    for k in range(4):
        w = pl.ds(k * SLICE, SLICE)
        copies.append(pltpu.make_async_copy(att.at[w], att_hbm.at[w], sem.at[1 + k]))
        copies.append(pltpu.make_async_copy(dq.at[w], dq_hbm.at[w], sem.at[5 + k]))
    for cp in copies:
        cp.start()
    for cp in copies:
        cp.wait()


def pinned(value):
    return pltpu.with_memory_space_constraint(value, pltpu.HBM)


def body(query, latent, segment, d_out):
    hbm = pl.BlockSpec(memory_space=pltpu.HBM)
    vspec = pl.BlockSpec(memory_space=pltpu.VMEM)
    V = pltpu.VMEM
    outs = (((TOK, HEADS * LAT), bf16), ((TOK, HEADS * WIDTH), bf16), ((TOK, WIDTH), f32))
    made = pl.pallas_call(
        kernel,
        out_shape=tuple(V(s, t) for s, t in outs),
        in_specs=[hbm, hbm, hbm, hbm],
        out_specs=(vspec, vspec, vspec),
        scratch_shapes=[
            V((PAIRS, TOK, 2 * WIDTH), bf16),
            V((PAIRS, TOK, 2 * LAT), bf16),
            V((3 * TOK, PADW), bf16),
            V((3 * TOK, PADW), bf16),
            V((2, PADW, WIN), bf16),
            V((2, PADW, WIN), bf16),
            V((2, WIN, 1536), bf16),
            V((2, WIN, 1536), bf16),
            V((12, 256, WIN), bf16),
            V((12, 256, WIN), bf16),
            V((128, WIN), f32),
            V((64, WIN), f32),
            V((3, 1, TOK), jnp.int32),
            V((2, 3 * TOK, PADW), f32),
            V((3 * TOK, WIDTH), f32),
            V((TOK, WIDTH), bf16),
            V((TOK, WIDTH), bf16),
            V((TOK, WIDTH), bf16),
            V((4, SLICE, WIDTH), bf16),
            V((TOK, WIDTH), bf16),
            V((3, SLICE, WIDTH), bf16),
            V((2, TOK, WIDTH), bf16),
            V((TOK, WIDTH), bf16),
            pltpu.SemaphoreType.DMA((2, PAIRS + 1)),
            pltpu.SemaphoreType.DMA((23,)),
            pltpu.SemaphoreType.DMA((23,)),
        ],
        compiler_params=pltpu.CompilerParams(
            collective_id=0, has_side_effects=True, vmem_limit_bytes=44 << 20
        ),
    )(pinned(query), pinned(latent), pinned(segment.reshape(1, TOK)), pinned(d_out))
    return pl.pallas_call(
        write_out,
        out_shape=tuple(jax.ShapeDtypeStruct(s, t) for s, t in outs),
        in_specs=[pl.BlockSpec(memory_space=pl.ANY)] * 3,
        out_specs=(hbm, hbm, hbm),
        scratch_shapes=[pltpu.SemaphoreType.DMA((9,))],
        compiler_params=pltpu.CompilerParams(vmem_limit_bytes=1 << 20),
    )(*made)


def solution(mesh):
    in_specs = (P("ctx", "head"), P("ctx", None), P("ctx"), P("ctx", "head"))
    out_specs = (P("ctx", "head"), P("ctx", "head"), P("ctx", None))
    return jax.shard_map(body, mesh=mesh, in_specs=in_specs, out_specs=out_specs, check_vma=False)
```

```python
import jax
import jax.numpy as jnp
from jax import lax
from jax.experimental import pallas as pl
from jax.experimental.pallas import tpu as pltpu
from jax.sharding import PartitionSpec as P

TOK = 192
HEADS = 16
PAIRS = HEADS // 2
LAT = 512
WIDTH = 576
PADW = 640
WIN = 512
NCTX = 32
SLICE = 48
HALF = 96
SCALE = 192.0 ** -0.5
SCALE2 = SCALE * 1.4426950408889634
bf16 = jnp.bfloat16
f32 = jnp.float32
MESH = pl.DeviceIdType.MESH

GROUPS = ((0, 0, 128, 2, 4, 0), (64, 128, 64, 4, 2, 8))


def dot(a, b):
    return jnp.dot(a, b, preferred_element_type=f32)


def remote(src, dst, send, recv, ctx, head):
    return pltpu.make_async_remote_copy(
        src_ref=src,
        dst_ref=dst,
        send_sem=send,
        recv_sem=recv,
        device_id={"ctx": ctx, "head": head},
        device_id_type=MESH,
    )


def kernel(
    q_hbm, lat_hbm, seg_hbm, do_hbm,
    att, dq, dl,
    q, do, ke, ko, kte, kto, pst, dst, p, ds, bias0, bias1, segs,
    acc, hsum, xs_send, xs_recv, zb_send, zb_recv, kb_recv, ob_send, ob_recv, tb, lat,
    in_sem, send_sem, recv_sem,
):
    here = lax.axis_index("ctx")
    head = lax.axis_index("head")
    y = head // 2
    c = lax.rem(head, 2)
    sib = y * 2 + 1 - c

    def at(d, core):
        return lax.rem(y + d, 4) * 2 + core

    has_next = here + 1 < NCTX
    has_prev = here >= 1
    has_two = here >= 2
    relays = jnp.logical_and(has_next, has_prev)
    nxt = jnp.minimum(here + 1, NCTX - 1)
    prv = jnp.maximum(here - 1, 0)
    first = c == 0
    second = c == 1

    barrier = pltpu.get_barrier_semaphore()

    def greet(ctx, hd):
        pl.semaphore_signal(barrier, inc=1, device_id={"ctx": ctx, "head": hd}, device_id_type=MESH)

    @pl.when(has_prev)
    def _():
        greet(prv, head)

    @pl.when(first)
    def _():
        @pl.when(has_next)
        def _():
            for d in range(4):
                greet(nxt, at(d, 0))

        @pl.when(relays)
        def _():
            greet(nxt, at(0, 1))

        for d in range(4):
            greet(here, at(d, 1))
        for d in range(1, 4):
            greet(here, at(d, 0))

    @pl.when(second)
    def _():
        for d in range(4):
            greet(here, at(d, 0))

    get_lat = pltpu.make_async_copy(lat_hbm, lat, in_sem.at[0, PAIRS])
    get_seg = pltpu.make_async_copy(seg_hbm, segs.at[2], in_sem.at[1, PAIRS])
    get_lat.start()
    get_seg.start()

    def rows(base, size):
        return pl.ds(pl.multiple_of(base, 16), size)

    get_seg.wait()
    get_lat.wait()
    ke[2 * TOK :, :] = jnp.concatenate([lat[...], jnp.zeros((TOK, PADW - WIDTH), bf16)], 1)

    @pl.when(jnp.logical_not(has_prev))
    def _():
        ke[TOK : 2 * TOK, :] = jnp.zeros((TOK, PADW), bf16)
        segs[1] = jnp.full((1, TOK), -1, jnp.int32)

    @pl.when(jnp.logical_not(has_two))
    def _():
        ke[:TOK, :] = jnp.zeros((TOK, PADW), bf16)
        segs[0] = jnp.full((1, TOK), -1, jnp.int32)

    one = has_next.astype(jnp.int32)
    two = has_prev.astype(jnp.int32)
    far = has_two.astype(jnp.int32)
    pl.semaphore_wait(barrier, one + (1 - c) * (4 * two + 7) + c * (far + 4))

    def halo(k):
        w = c * HALF + k * SLICE
        return remote(
            ke.at[rows(2 * TOK + w, SLICE)], ke.at[rows(TOK + w, SLICE)],
            send_sem.at[k], recv_sem.at[k], nxt, head,
        )

    def relay(k):
        w = c * HALF + k * SLICE
        return remote(
            ke.at[rows(TOK + w, SLICE)], ke.at[rows(w, SLICE)],
            send_sem.at[2 + k], recv_sem.at[2 + k], nxt, head,
        )

    def across(k, blk, core):
        w = rows(blk * TOK + core * HALF + k * SLICE, SLICE)
        i = 6 - 2 * blk + k
        return remote(ke.at[w], ke.at[w], send_sem.at[i], recv_sem.at[i], here, sib)

    seg_halo = remote(segs.at[2], segs.at[1], send_sem.at[8], recv_sem.at[8], nxt, head)
    seg_relay = remote(segs.at[1], segs.at[0], send_sem.at[9], recv_sem.at[9], nxt, head)

    @pl.when(has_next)
    def _():
        for k in range(2):
            halo(k).start()
        seg_halo.start()

    for i in range(PAIRS):
        pltpu.make_async_copy(
            q_hbm.at[:, pl.ds(2 * WIDTH * i, 2 * WIDTH)], q.at[i], in_sem.at[0, i]
        ).start()
        pltpu.make_async_copy(
            do_hbm.at[:, pl.ds(2 * LAT * i, 2 * LAT)], do.at[i], in_sem.at[1, i]
        ).start()

    @pl.when(has_prev)
    def _():
        for k in range(2):
            halo(k).wait_recv()

            @pl.when(has_next)
            def _():
                relay(k).start()

            across(k, 1, c).start()
        seg_halo.wait_recv()

        @pl.when(has_next)
        def _():
            seg_relay.start()

    @pl.when(has_two)
    def _():
        for k in range(2):
            relay(k).wait_recv()
            across(k, 0, c).start()
        seg_relay.wait_recv()

    seg_keys = jnp.broadcast_to(jnp.concatenate([segs[0], segs[1], segs[2]], 1), (TOK, 3 * TOK))
    tok = lax.broadcasted_iota(jnp.int32, (TOK, 3 * TOK), 0) + 2 * TOK
    key = lax.broadcasted_iota(jnp.int32, (TOK, 3 * TOK), 1)
    seg_q = jnp.sum(jnp.where(tok == key, seg_keys, 0), 1, keepdims=True)
    bias = jnp.where((seg_q == seg_keys) & (key <= tok), 0.0, -1e30)
    bias0[...] = bias[:128, :WIN]
    bias1[...] = bias[128:, 64:]

    @pl.when(has_prev)
    def _():
        for k in range(2):
            across(k, 1, 1 - c).wait_recv()

    @pl.when(has_two)
    def _():
        for k in range(2):
            across(k, 0, 1 - c).wait_recv()

    kev = ke[...]
    ko[...] = jnp.concatenate([jnp.zeros((3 * TOK, PADW - WIDTH), bf16), kev[:, :WIDTH]], 1)
    for g in (0, 1):
        st = GROUPS[g][0]
        kt = kev[st : st + WIN].T
        kte[g] = kt
        kto[g] = jnp.concatenate([jnp.zeros((PADW - WIDTH, WIN), bf16), kt[:WIDTH]], 0)

    def attend(g, i, par):
        _, t0, toks, n, _, first = GROUPS[g]
        bias_ref = (bias0, bias1)[g]
        qs = q[pl.ds(i * n, n), t0 : t0 + toks, par * LAT : par * LAT + PADW].reshape(256, PADW)
        os = do[pl.ds(i * n, n), t0 : t0 + toks, par * LAT : par * LAT + LAT].reshape(256, LAT)
        s = dot(qs, (kte, kto)[par][g])
        dp = dot(os, kte[g, :LAT, :])
        t = ((s * SCALE2).reshape(n, toks, WIN) + bias_ref[...][None]).reshape(256, WIN)
        e = jnp.exp2(t - jnp.max(t, 1, keepdims=True))
        pr = e * (1.0 / jnp.sum(e, 1, keepdims=True))
        delta = jnp.sum(pr * dp, 1, keepdims=True)
        d = (pr * (dp - delta) * SCALE).astype(bf16)
        pr = pr.astype(bf16)
        j = first + i * 2 + par
        p[j] = pr
        ds[j] = d
        cols = pl.ds(pl.multiple_of(g * 1024 + i * 256, 256), 256)
        pst[par, :, cols] = pr.T
        dst[par, :, cols] = d.T

    def wait_pair(i):
        pltpu.make_async_copy(
            q_hbm.at[:, pl.ds(0, 2 * WIDTH)], q.at[i], in_sem.at[0, i]
        ).wait()
        pltpu.make_async_copy(
            do_hbm.at[:, pl.ds(0, 2 * LAT)], do.at[i], in_sem.at[1, i]
        ).wait()

    for i in range(PAIRS):
        wait_pair(i)

    def step0(i, _):
        attend(0, i, 0)
        attend(0, i, 1)
        return 0

    def step1(i, _):
        attend(1, i, 0)
        attend(1, i, 1)
        return 0

    lax.fori_loop(0, 4, step0, 0, unroll=4)
    lax.fori_loop(0, 2, step1, 0, unroll=2)

    def key_grads(lo, hi):
        spans = ((0, lo, min(hi, WIN)), (1, max(lo, 64), hi))
        if hi > WIN:
            spans = spans[::-1]
        for at, (g, a, b) in enumerate(spans):
            st, t0, toks, _, _, _ = GROUPS[g]
            lanes = slice(g * 1024, g * 1024 + toks * PAIRS)
            w = slice(a - st, b - st)
            for par in (0, 1):
                qs = q[:, t0 : t0 + toks, par * LAT : par * LAT + PADW].reshape(toks * PAIRS, PADW)
                r = dot(dst[par, w, lanes], qs)
                acc[par, a:b] = r if at == 0 else acc[par, a:b] + r
            dv = sum(
                dot(
                    pst[par, w, lanes],
                    do[:, t0 : t0 + toks, par * LAT : par * LAT + LAT].reshape(toks * PAIRS, LAT),
                )
                for par in (0, 1)
            )
            acc[0, a:b, :LAT] += dv
        hsum[lo:hi] = acc[0, lo:hi, :WIDTH] + acc[1, lo:hi, PADW - WIDTH :]

    pair_sum = remote(xs_send, xs_recv, send_sem.at[10], recv_sem.at[10], here, sib)

    def chain(j):
        return remote(
            zb_send.at[pl.ds(j * SLICE, SLICE)], kb_recv.at[pl.ds(j * SLICE, SLICE)],
            send_sem.at[11 + j], recv_sem.at[11 + j], prv, at(0, 0),
        )

    def deliver(j, slot):
        return remote(
            zb_send.at[pl.ds(j * SLICE, SLICE)], zb_recv.at[slot],
            send_sem.at[15 + j], recv_sem.at[15 + slot], prv, j * 2,
        )

    def own_part(d, core):
        slot = d - 1 if core == 0 else 3 + d
        return remote(
            ob_send.at[rows(lax.rem(y + d, 4) * SLICE, SLICE)], ob_recv.at[slot],
            send_sem.at[19 + slot], recv_sem.at[19 + slot], here, at(d, 0),
        )

    key_grads(0, TOK)

    @pl.when(first)
    def _():
        xs_send[...] = hsum[:TOK].astype(bf16)
        pair_sum.start()

    key_grads(TOK, 2 * TOK)

    @pl.when(second)
    def _():
        xs_send[...] = hsum[TOK : 2 * TOK].astype(bf16)
        pair_sum.start()
        pair_sum.wait_recv()
        zb_send[...] = (hsum[:TOK] + xs_recv[...].astype(f32)).astype(bf16)

        @pl.when(has_two)
        def _():
            for j in range(4):
                chain(j).start()

    key_grads(2 * TOK, 3 * TOK)
    ob_send[...] = hsum[2 * TOK :].astype(bf16)

    @pl.when(first)
    def _():
        for d in (1, 3, 2):
            own_part(d, 0).start()
        pair_sum.wait_recv()
        hsum[TOK : 2 * TOK] += xs_recv[...].astype(f32)

    @pl.when(second)
    def _():
        for d in (1, 3, 2, 0):
            own_part(d, 1).start()

    def outputs(g, i):
        st, t0, toks, n, _, first = GROUPS[g]
        j = first + 2 * i
        for par in (0, 1):
            o = dot(p[j + par], ke[st : st + WIN, :LAT]).astype(bf16).reshape(n, toks, LAT)
            for a in range(n):
                col = (2 * (i * n + a) + par) * LAT
                att[t0 : t0 + toks, col : col + LAT] = o[a]
        qe = dot(ds[j], ke[st : st + WIN])
        qo = dot(ds[j + 1], ko[st : st + WIN])
        full = jnp.concatenate(
            [qe[:, :LAT], qe[:, LAT:] + qo[:, : PADW - LAT], qo[:, PADW - LAT :]], 1
        )
        full = full.astype(bf16).reshape(n, toks, 2 * WIDTH)
        for a in range(n):
            col = (i * n + a) * 2 * WIDTH
            dq[t0 : t0 + toks, col : col + 2 * WIDTH] = full[a]

    outputs(0, 0)
    outputs(0, 1)

    @pl.when(jnp.logical_and(first, has_prev))
    def _():
        for j in range(4):
            w = slice(j * SLICE, (j + 1) * SLICE)

            @pl.when(has_next)
            def _():
                chain(j).wait_recv()
                hsum[TOK + j * SLICE : TOK + (j + 1) * SLICE] += kb_recv[w].astype(f32)

            zb_send[w] = hsum[TOK + j * SLICE : TOK + (j + 1) * SLICE].astype(bf16)
            deliver(j, y).start()

    outputs(0, 2)
    outputs(0, 3)
    outputs(1, 0)
    outputs(1, 1)

    def share(d, core):
        w = rows(y * SLICE, SLICE)
        return remote(
            tb.at[w], tb.at[w], send_sem.at[26 + 4 * core + d], recv_sem.at[26 + y], here, at(d, core)
        )

    def shared(d):
        yy = lax.rem(y + d, 4)
        w = rows(yy * SLICE, SLICE)
        return remote(tb.at[w], tb.at[w], send_sem.at[26], recv_sem.at[26 + yy], here, sib)

    @pl.when(first)
    def _():
        for d in (1, 2, 3):
            own_part(d, 0).wait_recv()
        for d in range(4):
            own_part(d, 1).wait_recv()
        part = hsum[pl.ds(pl.multiple_of(2 * TOK + y * SLICE, 8), SLICE)]
        for k in range(7):
            part = part + ob_recv[k].astype(f32)
        hsum[:SLICE] = part

        @pl.when(has_next)
        def _():
            for k in range(4):
                deliver(k, k).wait_recv()
            got = zb_recv[0].astype(f32)
            for k in (1, 2, 3):
                got = got + zb_recv[k].astype(f32)
            hsum[:SLICE] += got

        tb[rows(y * SLICE, SLICE)] = hsum[:SLICE].astype(bf16)
        for d, core in ((1, 0), (1, 1), (3, 0), (3, 1), (2, 0), (2, 1), (0, 1)):
            share(d, core).start()
        for d in (1, 3, 2):
            shared(d).wait_recv()

    @pl.when(second)
    def _():
        for d in range(4):
            shared(d).wait_recv()

    dl[...] = tb[...].astype(f32)

    @pl.when(has_next)
    def _():
        for k in range(2):
            halo(k).wait_send()
        seg_halo.wait_send()

    @pl.when(has_prev)
    def _():
        for k in range(2):
            across(k, 1, c).wait_send()

    @pl.when(relays)
    def _():
        for k in range(2):
            relay(k).wait_send()
        seg_relay.wait_send()

    @pl.when(has_two)
    def _():
        for k in range(2):
            across(k, 0, c).wait_send()

    pair_sum.wait_send()

    @pl.when(first)
    def _():
        for d in (1, 3, 2):
            own_part(d, 0).wait_send()

        @pl.when(has_prev)
        def _():
            for j in range(4):
                deliver(j, y).wait_send()

        for d, core in ((1, 0), (1, 1), (3, 0), (3, 1), (2, 0), (2, 1), (0, 1)):
            share(d, core).wait_send()

    @pl.when(second)
    def _():
        for d in range(4):
            own_part(d, 1).wait_send()

        @pl.when(has_two)
        def _():
            for j in range(4):
                chain(j).wait_send()


def write_out(att, dq, dl, att_hbm, dq_hbm, dl_hbm, sem):
    copies = [pltpu.make_async_copy(dl, dl_hbm, sem.at[0])]
    for k in range(4):
        w = pl.ds(k * SLICE, SLICE)
        copies.append(pltpu.make_async_copy(att.at[w], att_hbm.at[w], sem.at[1 + k]))
        copies.append(pltpu.make_async_copy(dq.at[w], dq_hbm.at[w], sem.at[5 + k]))
    for cp in copies:
        cp.start()
    for cp in copies:
        cp.wait()


def pinned(value):
    return pltpu.with_memory_space_constraint(value, pltpu.HBM)


def body(query, latent, segment, d_out):
    hbm = pl.BlockSpec(memory_space=pltpu.HBM)
    vspec = pl.BlockSpec(memory_space=pltpu.VMEM)
    V = pltpu.VMEM
    outs = (((TOK, HEADS * LAT), bf16), ((TOK, HEADS * WIDTH), bf16), ((TOK, WIDTH), f32))
    made = pl.pallas_call(
        kernel,
        out_shape=tuple(V(s, t) for s, t in outs),
        in_specs=[hbm, hbm, hbm, hbm],
        out_specs=(vspec, vspec, vspec),
        scratch_shapes=[
            V((PAIRS, TOK, 2 * WIDTH), bf16),
            V((PAIRS, TOK, 2 * LAT), bf16),
            V((3 * TOK, PADW), bf16),
            V((3 * TOK, PADW), bf16),
            V((2, PADW, WIN), bf16),
            V((2, PADW, WIN), bf16),
            V((2, WIN, 1536), bf16),
            V((2, WIN, 1536), bf16),
            V((12, 256, WIN), bf16),
            V((12, 256, WIN), bf16),
            V((128, WIN), f32),
            V((64, WIN), f32),
            V((3, 1, TOK), jnp.int32),
            V((2, 3 * TOK, PADW), f32),
            V((3 * TOK, WIDTH), f32),
            V((TOK, WIDTH), bf16),
            V((TOK, WIDTH), bf16),
            V((TOK, WIDTH), bf16),
            V((4, SLICE, WIDTH), bf16),
            V((TOK, WIDTH), bf16),
            V((TOK, WIDTH), bf16),
            V((7, SLICE, WIDTH), bf16),
            V((TOK, WIDTH), bf16),
            V((TOK, WIDTH), bf16),
            pltpu.SemaphoreType.DMA((2, PAIRS + 1)),
            pltpu.SemaphoreType.DMA((34,)),
            pltpu.SemaphoreType.DMA((34,)),
        ],
        compiler_params=pltpu.CompilerParams(
            collective_id=0, has_side_effects=True, vmem_limit_bytes=44 << 20
        ),
    )(pinned(query), pinned(latent), pinned(segment.reshape(1, TOK)), pinned(d_out))
    return pl.pallas_call(
        write_out,
        out_shape=tuple(jax.ShapeDtypeStruct(s, t) for s, t in outs),
        in_specs=[pl.BlockSpec(memory_space=pl.ANY)] * 3,
        out_specs=(hbm, hbm, hbm),
        scratch_shapes=[pltpu.SemaphoreType.DMA((9,))],
        compiler_params=pltpu.CompilerParams(vmem_limit_bytes=1 << 20),
    )(*made)


def solution(mesh):
    in_specs = (P("ctx", "head"), P("ctx", None), P("ctx"), P("ctx", "head"))
    out_specs = (P("ctx", "head"), P("ctx", "head"), P("ctx", None))
    return jax.shard_map(body, mesh=mesh, in_specs=in_specs, out_specs=out_specs, check_vma=False)
```

```python
import jax
import jax.numpy as jnp
from jax import lax
from jax.experimental import pallas as pl
from jax.experimental.pallas import tpu as pltpu
from jax.sharding import PartitionSpec as P

TOK = 192
HEADS = 16
PAIRS = HEADS // 2
LAT = 512
WIDTH = 576
PADW = 640
WIN = 512
NCTX = 32
SLICE = 48
HALF = 96
SCALE = 192.0 ** -0.5
SCALE2 = SCALE * 1.4426950408889634
bf16 = jnp.bfloat16
f32 = jnp.float32
MESH = pl.DeviceIdType.MESH

GROUPS = ((0, 0, 128, 2, 4, 0), (64, 128, 64, 4, 2, 8))


def dot(a, b):
    return jnp.dot(a, b, preferred_element_type=f32)


def remote(src, dst, send, recv, ctx, head):
    return pltpu.make_async_remote_copy(
        src_ref=src,
        dst_ref=dst,
        send_sem=send,
        recv_sem=recv,
        device_id={"ctx": ctx, "head": head},
        device_id_type=MESH,
    )


def kernel(
    q_hbm, lat_hbm, seg_hbm, do_hbm,
    att, dq, dl,
    q, do, ke, ko, kte, kto, pst, dst, p, ds, bias0, bias1, segs,
    acc, hsum, xs_send, xs_recv, zb_send, zb_recv, kb_recv, ob_send, ob_recv, tb, lat, t_up, dp_up,
    in_sem, send_sem, recv_sem,
):
    here = lax.axis_index("ctx")
    head = lax.axis_index("head")
    y = head // 2
    c = lax.rem(head, 2)
    sib = y * 2 + 1 - c

    def at(d, core):
        return lax.rem(y + d, 4) * 2 + core

    has_next = here + 1 < NCTX
    has_prev = here >= 1
    has_two = here >= 2
    relays = jnp.logical_and(has_next, has_prev)
    nxt = jnp.minimum(here + 1, NCTX - 1)
    prv = jnp.maximum(here - 1, 0)
    first = c == 0
    second = c == 1

    barrier = pltpu.get_barrier_semaphore()

    def greet(ctx, hd):
        pl.semaphore_signal(barrier, inc=1, device_id={"ctx": ctx, "head": hd}, device_id_type=MESH)

    @pl.when(has_prev)
    def _():
        greet(prv, head)

    @pl.when(first)
    def _():
        @pl.when(has_next)
        def _():
            for d in range(4):
                greet(nxt, at(d, 0))

        @pl.when(relays)
        def _():
            greet(nxt, at(0, 1))

        for d in range(4):
            greet(here, at(d, 1))
        for d in range(1, 4):
            greet(here, at(d, 0))

    @pl.when(second)
    def _():
        for d in range(4):
            greet(here, at(d, 0))

    get_lat = pltpu.make_async_copy(lat_hbm, lat, in_sem.at[0, PAIRS])
    get_seg = pltpu.make_async_copy(seg_hbm, segs.at[2], in_sem.at[1, PAIRS])
    get_lat.start()
    get_seg.start()

    def rows(base, size):
        return pl.ds(pl.multiple_of(base, 16), size)

    get_seg.wait()
    get_lat.wait()
    ke[2 * TOK :, :] = jnp.concatenate([lat[...], jnp.zeros((TOK, PADW - WIDTH), bf16)], 1)

    @pl.when(jnp.logical_not(has_prev))
    def _():
        ke[TOK : 2 * TOK, :] = jnp.zeros((TOK, PADW), bf16)
        segs[1] = jnp.full((1, TOK), -1, jnp.int32)

    @pl.when(jnp.logical_not(has_two))
    def _():
        ke[:TOK, :] = jnp.zeros((TOK, PADW), bf16)
        segs[0] = jnp.full((1, TOK), -1, jnp.int32)

    one = has_next.astype(jnp.int32)
    two = has_prev.astype(jnp.int32)
    far = has_two.astype(jnp.int32)
    pl.semaphore_wait(barrier, one + (1 - c) * (4 * two + 7) + c * (far + 4))

    def halo(k):
        w = c * HALF + k * SLICE
        return remote(
            ke.at[rows(2 * TOK + w, SLICE)], ke.at[rows(TOK + w, SLICE)],
            send_sem.at[k], recv_sem.at[k], nxt, head,
        )

    def relay(k):
        w = c * HALF + k * SLICE
        return remote(
            ke.at[rows(TOK + w, SLICE)], ke.at[rows(w, SLICE)],
            send_sem.at[2 + k], recv_sem.at[2 + k], nxt, head,
        )

    def across(k, blk, core):
        w = rows(blk * TOK + core * HALF + k * SLICE, SLICE)
        i = 6 - 2 * blk + k
        return remote(ke.at[w], ke.at[w], send_sem.at[i], recv_sem.at[i], here, sib)

    seg_halo = remote(segs.at[2], segs.at[1], send_sem.at[8], recv_sem.at[8], nxt, head)
    seg_relay = remote(segs.at[1], segs.at[0], send_sem.at[9], recv_sem.at[9], nxt, head)

    @pl.when(has_next)
    def _():
        for k in range(2):
            halo(k).start()
        seg_halo.start()

    for i in range(PAIRS):
        pltpu.make_async_copy(
            q_hbm.at[:, pl.ds(2 * WIDTH * i, 2 * WIDTH)], q.at[i], in_sem.at[0, i]
        ).start()
        pltpu.make_async_copy(
            do_hbm.at[:, pl.ds(2 * LAT * i, 2 * LAT)], do.at[i], in_sem.at[1, i]
        ).start()

    @pl.when(has_prev)
    def _():
        for k in range(2):
            halo(k).wait_recv()

            @pl.when(has_next)
            def _():
                relay(k).start()

            across(k, 1, c).start()
        seg_halo.wait_recv()

        @pl.when(has_next)
        def _():
            seg_relay.start()

    tok = lax.broadcasted_iota(jnp.int32, (TOK, 3 * TOK), 0) + 2 * TOK
    key = lax.broadcasted_iota(jnp.int32, (TOK, 3 * TOK), 1)

    def mask(seg_row):
        seg_keys = jnp.broadcast_to(seg_row, (TOK, 3 * TOK))
        seg_q = jnp.sum(jnp.where(tok == key, seg_keys, 0), 1, keepdims=True)
        return jnp.where((seg_q == seg_keys) & (key <= tok), 0.0, -1e30)

    def transposed(g, lo, hi):
        st = GROUPS[g][0]
        kt = ke[st + lo : st + hi].T
        kte[g, :, lo:hi] = kt
        kto[g, :, lo:hi] = jnp.concatenate(
            [jnp.zeros((PADW - WIDTH, hi - lo), bf16), kt[:WIDTH]], 0
        )

    def chunk(g, i, par):
        _, t0, toks, n, _, start = GROUPS[g]
        qs = q[pl.ds(i * n, n), t0 : t0 + toks, par * LAT : par * LAT + PADW].reshape(256, PADW)
        os = do[pl.ds(i * n, n), t0 : t0 + toks, par * LAT : par * LAT + LAT].reshape(256, LAT)
        return qs, os, start + i * 2 + par

    def scores(g, qs, par, w):
        _, _, toks, n, _, _ = GROUPS[g]
        s = dot(qs, (kte, kto)[par][g, :, w])
        bias = (bias0, bias1)[g][:, w]
        return ((s * SCALE2).reshape(n, toks, w.stop - w.start) + bias[None]).reshape(256, -1)

    UP = slice(WIN // 2, WIN)
    LOW = slice(0, WIN // 2)

    def upper(g, i, par):
        qs, os, j = chunk(g, i, par)
        t_up[j] = scores(g, qs, par, UP)
        dp_up[j] = dot(os, kte[g, :LAT, UP])

    def attend(g, i, par):
        qs, os, j = chunk(g, i, par)
        t = jnp.concatenate([scores(g, qs, par, LOW), t_up[j]], 1)
        dp = jnp.concatenate([dot(os, kte[g, :LAT, LOW]), dp_up[j]], 1)
        e = jnp.exp2(t - jnp.max(t, 1, keepdims=True))
        pr = e * (1.0 / jnp.sum(e, 1, keepdims=True))
        delta = jnp.sum(pr * dp, 1, keepdims=True)
        d = (pr * (dp - delta) * SCALE).astype(bf16)
        pr = pr.astype(bf16)
        p[j] = pr
        ds[j] = d
        cols = pl.ds(pl.multiple_of(g * 1024 + i * 256, 256), 256)
        pst[par, :, cols] = pr.T
        dst[par, :, cols] = d.T

    def wait_pair(i):
        pltpu.make_async_copy(
            q_hbm.at[:, pl.ds(0, 2 * WIDTH)], q.at[i], in_sem.at[0, i]
        ).wait()
        pltpu.make_async_copy(
            do_hbm.at[:, pl.ds(0, 2 * LAT)], do.at[i], in_sem.at[1, i]
        ).wait()

    @pl.when(has_prev)
    def _():
        for k in range(2):
            across(k, 1, 1 - c).wait_recv()

    near = mask(jnp.concatenate([jnp.full((1, TOK), -1, jnp.int32), segs[1], segs[2]], 1))
    bias0[:, UP] = near[:128, 256:WIN]
    bias1[:, UP] = near[128:, 320:]
    for g in (0, 1):
        transposed(g, 256, WIN)
    for i in range(PAIRS):
        wait_pair(i)

    def up0(i, _):
        upper(0, i, 0)
        upper(0, i, 1)
        return 0

    def up1(i, _):
        upper(1, i, 0)
        upper(1, i, 1)
        return 0

    lax.fori_loop(0, 4, up0, 0, unroll=4)
    lax.fori_loop(0, 2, up1, 0, unroll=2)

    @pl.when(has_two)
    def _():
        for k in range(2):
            relay(k).wait_recv()
            across(k, 0, c).start()
        seg_relay.wait_recv()

    full_mask = mask(jnp.concatenate([segs[0], segs[1], segs[2]], 1))
    bias0[:, LOW] = full_mask[:128, :256]
    bias1[:, LOW] = full_mask[128:, 64:320]

    @pl.when(has_two)
    def _():
        for k in range(2):
            across(k, 0, 1 - c).wait_recv()

    for g in (0, 1):
        transposed(g, 0, 256)
    ko[...] = jnp.concatenate([jnp.zeros((3 * TOK, PADW - WIDTH), bf16), ke[:, :WIDTH]], 1)

    def step0(i, _):
        attend(0, i, 0)
        attend(0, i, 1)
        return 0

    def step1(i, _):
        attend(1, i, 0)
        attend(1, i, 1)
        return 0

    lax.fori_loop(0, 4, step0, 0, unroll=4)
    lax.fori_loop(0, 2, step1, 0, unroll=2)

    def key_grads(lo, hi):
        spans = ((0, lo, min(hi, WIN)), (1, max(lo, 64), hi))
        if hi > WIN:
            spans = spans[::-1]
        for at, (g, a, b) in enumerate(spans):
            st, t0, toks, _, _, _ = GROUPS[g]
            lanes = slice(g * 1024, g * 1024 + toks * PAIRS)
            w = slice(a - st, b - st)
            for par in (0, 1):
                qs = q[:, t0 : t0 + toks, par * LAT : par * LAT + PADW].reshape(toks * PAIRS, PADW)
                r = dot(dst[par, w, lanes], qs)
                acc[par, a:b] = r if at == 0 else acc[par, a:b] + r
            dv = sum(
                dot(
                    pst[par, w, lanes],
                    do[:, t0 : t0 + toks, par * LAT : par * LAT + LAT].reshape(toks * PAIRS, LAT),
                )
                for par in (0, 1)
            )
            acc[0, a:b, :LAT] += dv
        hsum[lo:hi] = acc[0, lo:hi, :WIDTH] + acc[1, lo:hi, PADW - WIDTH :]

    pair_sum = remote(xs_send, xs_recv, send_sem.at[10], recv_sem.at[10], here, sib)

    def chain(j):
        return remote(
            zb_send.at[pl.ds(j * SLICE, SLICE)], kb_recv.at[pl.ds(j * SLICE, SLICE)],
            send_sem.at[11 + j], recv_sem.at[11 + j], prv, at(0, 0),
        )

    def deliver(j, slot):
        return remote(
            zb_send.at[pl.ds(j * SLICE, SLICE)], zb_recv.at[slot],
            send_sem.at[15 + j], recv_sem.at[15 + slot], prv, j * 2,
        )

    def own_part(d, core):
        slot = d - 1 if core == 0 else 3 + d
        return remote(
            ob_send.at[rows(lax.rem(y + d, 4) * SLICE, SLICE)], ob_recv.at[slot],
            send_sem.at[19 + slot], recv_sem.at[19 + slot], here, at(d, 0),
        )

    key_grads(0, TOK)

    @pl.when(first)
    def _():
        xs_send[...] = hsum[:TOK].astype(bf16)
        pair_sum.start()

    key_grads(TOK, 2 * TOK)

    @pl.when(second)
    def _():
        xs_send[...] = hsum[TOK : 2 * TOK].astype(bf16)
        pair_sum.start()
        pair_sum.wait_recv()
        zb_send[...] = (hsum[:TOK] + xs_recv[...].astype(f32)).astype(bf16)

        @pl.when(has_two)
        def _():
            for j in range(4):
                chain(j).start()

    key_grads(2 * TOK, 3 * TOK)
    ob_send[...] = hsum[2 * TOK :].astype(bf16)

    @pl.when(first)
    def _():
        for d in (1, 3, 2):
            own_part(d, 0).start()
        pair_sum.wait_recv()
        hsum[TOK : 2 * TOK] += xs_recv[...].astype(f32)

    @pl.when(second)
    def _():
        for d in (1, 3, 2, 0):
            own_part(d, 1).start()

    def outputs(g, i):
        st, t0, toks, n, _, first = GROUPS[g]
        j = first + 2 * i
        for par in (0, 1):
            o = dot(p[j + par], ke[st : st + WIN, :LAT]).astype(bf16).reshape(n, toks, LAT)
            for a in range(n):
                col = (2 * (i * n + a) + par) * LAT
                att[t0 : t0 + toks, col : col + LAT] = o[a]
        qe = dot(ds[j], ke[st : st + WIN])
        qo = dot(ds[j + 1], ko[st : st + WIN])
        full = jnp.concatenate(
            [qe[:, :LAT], qe[:, LAT:] + qo[:, : PADW - LAT], qo[:, PADW - LAT :]], 1
        )
        full = full.astype(bf16).reshape(n, toks, 2 * WIDTH)
        for a in range(n):
            col = (i * n + a) * 2 * WIDTH
            dq[t0 : t0 + toks, col : col + 2 * WIDTH] = full[a]


    outputs(0, 0)

    @pl.when(jnp.logical_and(first, has_prev))
    def _():
        for j in range(4):
            w = slice(j * SLICE, (j + 1) * SLICE)

            @pl.when(has_next)
            def _():
                chain(j).wait_recv()
                hsum[TOK + j * SLICE : TOK + (j + 1) * SLICE] += kb_recv[w].astype(f32)

            zb_send[w] = hsum[TOK + j * SLICE : TOK + (j + 1) * SLICE].astype(bf16)
            deliver(j, y).start()


    outputs(0, 1)
    outputs(0, 2)

    def share(d, core):
        w = rows(y * SLICE, SLICE)
        return remote(
            tb.at[w], tb.at[w], send_sem.at[26 + 4 * core + d], recv_sem.at[26 + y], here, at(d, core)
        )

    def shared(d):
        yy = lax.rem(y + d, 4)
        w = rows(yy * SLICE, SLICE)
        return remote(tb.at[w], tb.at[w], send_sem.at[26], recv_sem.at[26 + yy], here, sib)

    @pl.when(first)
    def _():
        for d in (1, 2, 3):
            own_part(d, 0).wait_recv()
        for d in range(4):
            own_part(d, 1).wait_recv()
        part = hsum[pl.ds(pl.multiple_of(2 * TOK + y * SLICE, 8), SLICE)]
        for k in range(7):
            part = part + ob_recv[k].astype(f32)
        hsum[:SLICE] = part

        @pl.when(has_next)
        def _():
            for k in range(4):
                deliver(k, k).wait_recv()
            got = zb_recv[0].astype(f32)
            for k in (1, 2, 3):
                got = got + zb_recv[k].astype(f32)
            hsum[:SLICE] += got

        tb[rows(y * SLICE, SLICE)] = hsum[:SLICE].astype(bf16)
        for d, core in ((1, 0), (1, 1), (3, 0), (3, 1), (2, 0), (2, 1), (0, 1)):
            share(d, core).start()

    outputs(0, 3)
    outputs(1, 0)
    outputs(1, 1)

    @pl.when(first)
    def _():
        for d in (1, 3, 2):
            shared(d).wait_recv()

    @pl.when(second)
    def _():
        for d in range(4):
            shared(d).wait_recv()

    dl[...] = tb[...].astype(f32)

    @pl.when(has_next)
    def _():
        for k in range(2):
            halo(k).wait_send()
        seg_halo.wait_send()

    @pl.when(has_prev)
    def _():
        for k in range(2):
            across(k, 1, c).wait_send()

    @pl.when(relays)
    def _():
        for k in range(2):
            relay(k).wait_send()
        seg_relay.wait_send()

    @pl.when(has_two)
    def _():
        for k in range(2):
            across(k, 0, c).wait_send()

    pair_sum.wait_send()

    @pl.when(first)
    def _():
        for d in (1, 3, 2):
            own_part(d, 0).wait_send()

        @pl.when(has_prev)
        def _():
            for j in range(4):
                deliver(j, y).wait_send()

        for d, core in ((1, 0), (1, 1), (3, 0), (3, 1), (2, 0), (2, 1), (0, 1)):
            share(d, core).wait_send()

    @pl.when(second)
    def _():
        for d in range(4):
            own_part(d, 1).wait_send()

        @pl.when(has_two)
        def _():
            for j in range(4):
                chain(j).wait_send()


def write_out(att, dq, dl, att_hbm, dq_hbm, dl_hbm, sem):
    copies = [pltpu.make_async_copy(dl, dl_hbm, sem.at[0])]
    for k in range(4):
        w = pl.ds(k * SLICE, SLICE)
        copies.append(pltpu.make_async_copy(att.at[w], att_hbm.at[w], sem.at[1 + k]))
        copies.append(pltpu.make_async_copy(dq.at[w], dq_hbm.at[w], sem.at[5 + k]))
    for cp in copies:
        cp.start()
    for cp in copies:
        cp.wait()


def pinned(value):
    return pltpu.with_memory_space_constraint(value, pltpu.HBM)


def body(query, latent, segment, d_out):
    hbm = pl.BlockSpec(memory_space=pltpu.HBM)
    vspec = pl.BlockSpec(memory_space=pltpu.VMEM)
    V = pltpu.VMEM
    outs = (((TOK, HEADS * LAT), bf16), ((TOK, HEADS * WIDTH), bf16), ((TOK, WIDTH), f32))
    made = pl.pallas_call(
        kernel,
        out_shape=tuple(V(s, t) for s, t in outs),
        in_specs=[hbm, hbm, hbm, hbm],
        out_specs=(vspec, vspec, vspec),
        scratch_shapes=[
            V((PAIRS, TOK, 2 * WIDTH), bf16),
            V((PAIRS, TOK, 2 * LAT), bf16),
            V((3 * TOK, PADW), bf16),
            V((3 * TOK, PADW), bf16),
            V((2, PADW, WIN), bf16),
            V((2, PADW, WIN), bf16),
            V((2, WIN, 1536), bf16),
            V((2, WIN, 1536), bf16),
            V((12, 256, WIN), bf16),
            V((12, 256, WIN), bf16),
            V((128, WIN), f32),
            V((64, WIN), f32),
            V((3, 1, TOK), jnp.int32),
            V((2, 3 * TOK, PADW), f32),
            V((3 * TOK, WIDTH), f32),
            V((TOK, WIDTH), bf16),
            V((TOK, WIDTH), bf16),
            V((TOK, WIDTH), bf16),
            V((4, SLICE, WIDTH), bf16),
            V((TOK, WIDTH), bf16),
            V((TOK, WIDTH), bf16),
            V((7, SLICE, WIDTH), bf16),
            V((TOK, WIDTH), bf16),
            V((TOK, WIDTH), bf16),
            V((12, 256, WIN // 2), f32),
            V((12, 256, WIN // 2), f32),
            pltpu.SemaphoreType.DMA((2, PAIRS + 1)),
            pltpu.SemaphoreType.DMA((34,)),
            pltpu.SemaphoreType.DMA((34,)),
        ],
        compiler_params=pltpu.CompilerParams(
            collective_id=0, has_side_effects=True, vmem_limit_bytes=50 << 20
        ),
    )(pinned(query), pinned(latent), pinned(segment.reshape(1, TOK)), pinned(d_out))
    return pl.pallas_call(
        write_out,
        out_shape=tuple(jax.ShapeDtypeStruct(s, t) for s, t in outs),
        in_specs=[pl.BlockSpec(memory_space=pl.ANY)] * 3,
        out_specs=(hbm, hbm, hbm),
        scratch_shapes=[pltpu.SemaphoreType.DMA((9,))],
        compiler_params=pltpu.CompilerParams(vmem_limit_bytes=1 << 20),
    )(*made)


def solution(mesh):
    in_specs = (P("ctx", "head"), P("ctx", None), P("ctx"), P("ctx", "head"))
    out_specs = (P("ctx", "head"), P("ctx", "head"), P("ctx", None))
    return jax.shard_map(body, mesh=mesh, in_specs=in_specs, out_specs=out_specs, check_vma=False)
```

```python
import jax
import jax.numpy as jnp
from jax import lax
from jax.experimental import pallas as pl
from jax.experimental.pallas import tpu as pltpu
from jax.sharding import PartitionSpec as P

TOK = 192
HEADS = 16
PAIRS = HEADS // 2
LAT = 512
WIDTH = 576
PADW = 640
WIN = 512
NCTX = 32
SLICE = 48
HALF = 96
SCALE = 192.0 ** -0.5
SCALE2 = SCALE * 1.4426950408889634
bf16 = jnp.bfloat16
f32 = jnp.float32
MESH = pl.DeviceIdType.MESH

GROUPS = ((0, 0, 128, 2, 4, 0), (64, 128, 64, 4, 2, 8))


def dot(a, b):
    return jnp.dot(a, b, preferred_element_type=f32)


def remote(src, dst, send, recv, ctx, head):
    return pltpu.make_async_remote_copy(
        src_ref=src,
        dst_ref=dst,
        send_sem=send,
        recv_sem=recv,
        device_id={"ctx": ctx, "head": head},
        device_id_type=MESH,
    )


def kernel(
    q_hbm, lat_hbm, seg_hbm, do_hbm,
    att, dq, dl,
    q, do, ke, ko, kte, kto, pst, dst, p, ds, bias0, bias1, segs,
    acc, hsum, xs_send, xs_recv, zb_send, zb_recv, kb_recv, ob_send, ob_recv, tb, lat, t_up, dp_up,
    in_sem, send_sem, recv_sem,
):
    here = lax.axis_index("ctx")
    head = lax.axis_index("head")
    y = head // 2
    c = lax.rem(head, 2)
    sib = y * 2 + 1 - c

    def at(d, core):
        return lax.rem(y + d, 4) * 2 + core

    has_next = here + 1 < NCTX
    has_prev = here >= 1
    has_two = here >= 2
    relays = jnp.logical_and(has_next, has_prev)
    nxt = jnp.minimum(here + 1, NCTX - 1)
    prv = jnp.maximum(here - 1, 0)
    first = c == 0
    second = c == 1

    get_lat = pltpu.make_async_copy(lat_hbm, lat, in_sem.at[0, PAIRS])
    get_seg = pltpu.make_async_copy(seg_hbm, segs.at[2], in_sem.at[1, PAIRS])
    get_lat.start()
    get_seg.start()

    barrier = pltpu.get_barrier_semaphore()

    def greet(ctx, hd):
        pl.semaphore_signal(barrier, inc=1, device_id={"ctx": ctx, "head": hd}, device_id_type=MESH)

    @pl.when(has_prev)
    def _():
        greet(prv, head)

    @pl.when(first)
    def _():
        @pl.when(has_next)
        def _():
            for d in range(4):
                greet(nxt, at(d, 0))

        @pl.when(relays)
        def _():
            greet(nxt, at(0, 1))

        for d in range(4):
            greet(here, at(d, 1))
        for d in range(1, 4):
            greet(here, at(d, 0))

    @pl.when(second)
    def _():
        for d in range(4):
            greet(here, at(d, 0))

    def rows(base, size):
        return pl.ds(pl.multiple_of(base, 16), size)

    get_seg.wait()
    get_lat.wait()
    ke[2 * TOK :, :] = jnp.concatenate([lat[...], jnp.zeros((TOK, PADW - WIDTH), bf16)], 1)

    @pl.when(jnp.logical_not(has_prev))
    def _():
        ke[TOK : 2 * TOK, :] = jnp.zeros((TOK, PADW), bf16)
        segs[1] = jnp.full((1, TOK), -1, jnp.int32)

    @pl.when(jnp.logical_not(has_two))
    def _():
        ke[:TOK, :] = jnp.zeros((TOK, PADW), bf16)
        segs[0] = jnp.full((1, TOK), -1, jnp.int32)

    one = has_next.astype(jnp.int32)
    two = has_prev.astype(jnp.int32)
    far = has_two.astype(jnp.int32)
    pl.semaphore_wait(barrier, one + (1 - c) * (4 * two + 7) + c * (far + 4))

    def halo(k):
        w = c * HALF + k * SLICE
        return remote(
            ke.at[rows(2 * TOK + w, SLICE)], ke.at[rows(TOK + w, SLICE)],
            send_sem.at[k], recv_sem.at[k], nxt, head,
        )

    def relay(k):
        w = c * HALF + k * SLICE
        return remote(
            ke.at[rows(TOK + w, SLICE)], ke.at[rows(w, SLICE)],
            send_sem.at[2 + k], recv_sem.at[2 + k], nxt, head,
        )

    def across(k, blk, core):
        w = rows(blk * TOK + core * HALF + k * SLICE, SLICE)
        i = 6 - 2 * blk + k
        return remote(ke.at[w], ke.at[w], send_sem.at[i], recv_sem.at[i], here, sib)

    seg_halo = remote(segs.at[2], segs.at[1], send_sem.at[8], recv_sem.at[8], nxt, head)
    seg_relay = remote(segs.at[1], segs.at[0], send_sem.at[9], recv_sem.at[9], nxt, head)

    @pl.when(has_next)
    def _():
        for k in range(2):
            halo(k).start()
        seg_halo.start()

    for i in range(PAIRS):
        pltpu.make_async_copy(
            q_hbm.at[:, pl.ds(2 * WIDTH * i, 2 * WIDTH)], q.at[i], in_sem.at[0, i]
        ).start()
        pltpu.make_async_copy(
            do_hbm.at[:, pl.ds(2 * LAT * i, 2 * LAT)], do.at[i], in_sem.at[1, i]
        ).start()

    @pl.when(has_prev)
    def _():
        for k in range(2):
            halo(k).wait_recv()

            @pl.when(has_next)
            def _():
                relay(k).start()

            across(k, 1, c).start()
        seg_halo.wait_recv()

        @pl.when(has_next)
        def _():
            seg_relay.start()

    tok = lax.broadcasted_iota(jnp.int32, (TOK, 3 * TOK), 0) + 2 * TOK
    key = lax.broadcasted_iota(jnp.int32, (TOK, 3 * TOK), 1)

    def mask(seg_row):
        seg_keys = jnp.broadcast_to(seg_row, (TOK, 3 * TOK))
        seg_q = jnp.sum(jnp.where(tok == key, seg_keys, 0), 1, keepdims=True)
        return jnp.where((seg_q == seg_keys) & (key <= tok), 0.0, -1e30)

    def transposed(g, lo, hi):
        st = GROUPS[g][0]
        kt = ke[st + lo : st + hi].T
        kte[g, :, lo:hi] = kt
        kto[g, :, lo:hi] = jnp.concatenate(
            [jnp.zeros((PADW - WIDTH, hi - lo), bf16), kt[:WIDTH]], 0
        )

    def chunk(g, i, par):
        _, t0, toks, n, _, start = GROUPS[g]
        qs = q[pl.ds(i * n, n), t0 : t0 + toks, par * LAT : par * LAT + PADW].reshape(256, PADW)
        os = do[pl.ds(i * n, n), t0 : t0 + toks, par * LAT : par * LAT + LAT].reshape(256, LAT)
        return qs, os, start + i * 2 + par

    def scores(g, qs, par, w):
        _, _, toks, n, _, _ = GROUPS[g]
        s = dot(qs, (kte, kto)[par][g, :, w])
        bias = (bias0, bias1)[g][:, w]
        return ((s * SCALE2).reshape(n, toks, w.stop - w.start) + bias[None]).reshape(256, -1)

    UP = slice(WIN // 2, WIN)
    LOW = slice(0, WIN // 2)

    def upper(g, i, par):
        qs, os, j = chunk(g, i, par)
        t_up[j] = scores(g, qs, par, UP)
        dp_up[j] = dot(os, kte[g, :LAT, UP])

    def attend(g, i, par):
        qs, os, j = chunk(g, i, par)
        t = jnp.concatenate([scores(g, qs, par, LOW), t_up[j]], 1)
        dp = jnp.concatenate([dot(os, kte[g, :LAT, LOW]), dp_up[j]], 1)
        e = jnp.exp2(t - jnp.max(t, 1, keepdims=True))
        pr = e * (1.0 / jnp.sum(e, 1, keepdims=True))
        delta = jnp.sum(pr * dp, 1, keepdims=True)
        d = (pr * (dp - delta) * SCALE).astype(bf16)
        pr = pr.astype(bf16)
        p[j] = pr
        ds[j] = d
        cols = pl.ds(pl.multiple_of(g * 1024 + i * 256, 256), 256)
        pst[par, :, cols] = pr.T
        dst[par, :, cols] = d.T

    def wait_pair(i):
        pltpu.make_async_copy(
            q_hbm.at[:, pl.ds(0, 2 * WIDTH)], q.at[i], in_sem.at[0, i]
        ).wait()
        pltpu.make_async_copy(
            do_hbm.at[:, pl.ds(0, 2 * LAT)], do.at[i], in_sem.at[1, i]
        ).wait()

    @pl.when(has_prev)
    def _():
        for k in range(2):
            across(k, 1, 1 - c).wait_recv()

    near = mask(jnp.concatenate([jnp.full((1, TOK), -1, jnp.int32), segs[1], segs[2]], 1))
    bias0[:, UP] = near[:128, 256:WIN]
    bias1[:, UP] = near[128:, 320:]
    for g in (0, 1):
        transposed(g, 256, WIN)
    for i in range(PAIRS):
        wait_pair(i)

    def up0(i, _):
        upper(0, i, 0)
        upper(0, i, 1)
        return 0

    def up1(i, _):
        upper(1, i, 0)
        upper(1, i, 1)
        return 0

    lax.fori_loop(0, 4, up0, 0, unroll=4)
    lax.fori_loop(0, 2, up1, 0, unroll=2)

    @pl.when(has_two)
    def _():
        for k in range(2):
            relay(k).wait_recv()
            across(k, 0, c).start()
        seg_relay.wait_recv()

    full_mask = mask(jnp.concatenate([segs[0], segs[1], segs[2]], 1))
    bias0[:, LOW] = full_mask[:128, :256]
    bias1[:, LOW] = full_mask[128:, 64:320]

    @pl.when(has_two)
    def _():
        for k in range(2):
            across(k, 0, 1 - c).wait_recv()

    for g in (0, 1):
        transposed(g, 0, 256)
    ko[...] = jnp.concatenate([jnp.zeros((3 * TOK, PADW - WIDTH), bf16), ke[:, :WIDTH]], 1)

    def step0(i, _):
        attend(0, i, 0)
        attend(0, i, 1)
        return 0

    def step1(i, _):
        attend(1, i, 0)
        attend(1, i, 1)
        return 0

    lax.fori_loop(0, 4, step0, 0, unroll=4)
    lax.fori_loop(0, 2, step1, 0, unroll=2)

    def key_grads(lo, hi):
        spans = ((0, lo, min(hi, WIN)), (1, max(lo, 64), hi))
        if hi > WIN:
            spans = spans[::-1]
        for at, (g, a, b) in enumerate(spans):
            st, t0, toks, _, _, _ = GROUPS[g]
            lanes = slice(g * 1024, g * 1024 + toks * PAIRS)
            w = slice(a - st, b - st)
            for par in (0, 1):
                qs = q[:, t0 : t0 + toks, par * LAT : par * LAT + PADW].reshape(toks * PAIRS, PADW)
                r = dot(dst[par, w, lanes], qs)
                acc[par, a:b] = r if at == 0 else acc[par, a:b] + r
            dv = sum(
                dot(
                    pst[par, w, lanes],
                    do[:, t0 : t0 + toks, par * LAT : par * LAT + LAT].reshape(toks * PAIRS, LAT),
                )
                for par in (0, 1)
            )
            acc[0, a:b, :LAT] += dv
        hsum[lo:hi] = acc[0, lo:hi, :WIDTH] + acc[1, lo:hi, PADW - WIDTH :]

    pair_sum = remote(xs_send, xs_recv, send_sem.at[10], recv_sem.at[10], here, sib)

    def chain(j):
        return remote(
            zb_send.at[pl.ds(j * SLICE, SLICE)], kb_recv.at[pl.ds(j * SLICE, SLICE)],
            send_sem.at[11 + j], recv_sem.at[11 + j], prv, at(0, 0),
        )

    def deliver(j, slot):
        return remote(
            zb_send.at[pl.ds(j * SLICE, SLICE)], zb_recv.at[slot],
            send_sem.at[15 + j], recv_sem.at[15 + slot], prv, j * 2,
        )

    def own_part(d, core):
        slot = d - 1 if core == 0 else 3 + d
        return remote(
            ob_send.at[rows(lax.rem(y + d, 4) * SLICE, SLICE)], ob_recv.at[slot],
            send_sem.at[19 + slot], recv_sem.at[19 + slot], here, at(d, 0),
        )

    key_grads(0, 2 * TOK)
    xs_send[...] = hsum[rows(c * TOK, TOK)].astype(bf16)
    pair_sum.start()

    @pl.when(second)
    def _():
        pair_sum.wait_recv()
        zb_send[...] = (hsum[:TOK] + xs_recv[...].astype(f32)).astype(bf16)

        @pl.when(has_two)
        def _():
            for j in range(4):
                chain(j).start()

    key_grads(2 * TOK, 3 * TOK)
    ob_send[...] = hsum[2 * TOK :].astype(bf16)

    @pl.when(first)
    def _():
        for d in (1, 3, 2):
            own_part(d, 0).start()
        pair_sum.wait_recv()
        hsum[TOK : 2 * TOK] += xs_recv[...].astype(f32)

    @pl.when(second)
    def _():
        for d in (1, 3, 2, 0):
            own_part(d, 1).start()

    def outputs(g, i):
        st, t0, toks, n, _, first = GROUPS[g]
        j = first + 2 * i
        for par in (0, 1):
            o = dot(p[j + par], ke[st : st + WIN, :LAT]).astype(bf16).reshape(n, toks, LAT)
            for a in range(n):
                col = (2 * (i * n + a) + par) * LAT
                att[t0 : t0 + toks, col : col + LAT] = o[a]
        qe = dot(ds[j], ke[st : st + WIN])
        qo = dot(ds[j + 1], ko[st : st + WIN])
        full = jnp.concatenate(
            [qe[:, :LAT], qe[:, LAT:] + qo[:, : PADW - LAT], qo[:, PADW - LAT :]], 1
        )
        full = full.astype(bf16).reshape(n, toks, 2 * WIDTH)
        for a in range(n):
            col = (i * n + a) * 2 * WIDTH
            dq[t0 : t0 + toks, col : col + 2 * WIDTH] = full[a]


    outputs(0, 0)

    @pl.when(jnp.logical_and(first, has_prev))
    def _():
        for j in range(4):
            w = slice(j * SLICE, (j + 1) * SLICE)

            @pl.when(has_next)
            def _():
                chain(j).wait_recv()
                hsum[TOK + j * SLICE : TOK + (j + 1) * SLICE] += kb_recv[w].astype(f32)

            zb_send[w] = hsum[TOK + j * SLICE : TOK + (j + 1) * SLICE].astype(bf16)
            deliver(j, y).start()


    outputs(0, 1)
    outputs(0, 2)

    def share(d, core):
        w = rows(y * SLICE, SLICE)
        return remote(
            tb.at[w], tb.at[w], send_sem.at[26 + 4 * core + d], recv_sem.at[26 + y], here, at(d, core)
        )

    def shared(d):
        yy = lax.rem(y + d, 4)
        w = rows(yy * SLICE, SLICE)
        return remote(tb.at[w], tb.at[w], send_sem.at[26], recv_sem.at[26 + yy], here, sib)

    @pl.when(first)
    def _():
        for d in (1, 2, 3):
            own_part(d, 0).wait_recv()
        for d in range(4):
            own_part(d, 1).wait_recv()
        part = hsum[pl.ds(pl.multiple_of(2 * TOK + y * SLICE, 8), SLICE)]
        for k in range(7):
            part = part + ob_recv[k].astype(f32)
        hsum[:SLICE] = part

        @pl.when(has_next)
        def _():
            for k in range(4):
                deliver(k, k).wait_recv()
            got = zb_recv[0].astype(f32)
            for k in (1, 2, 3):
                got = got + zb_recv[k].astype(f32)
            hsum[:SLICE] += got

        tb[rows(y * SLICE, SLICE)] = hsum[:SLICE].astype(bf16)
        for d, core in ((1, 0), (1, 1), (3, 0), (3, 1), (2, 0), (2, 1), (0, 1)):
            share(d, core).start()

    outputs(0, 3)
    outputs(1, 0)
    outputs(1, 1)

    @pl.when(first)
    def _():
        for d in (1, 3, 2):
            shared(d).wait_recv()

    @pl.when(second)
    def _():
        for d in range(4):
            shared(d).wait_recv()

    dl[...] = tb[...].astype(f32)

    @pl.when(has_next)
    def _():
        for k in range(2):
            halo(k).wait_send()
        seg_halo.wait_send()

    @pl.when(has_prev)
    def _():
        for k in range(2):
            across(k, 1, c).wait_send()

    @pl.when(relays)
    def _():
        for k in range(2):
            relay(k).wait_send()
        seg_relay.wait_send()

    @pl.when(has_two)
    def _():
        for k in range(2):
            across(k, 0, c).wait_send()

    pair_sum.wait_send()

    @pl.when(first)
    def _():
        for d in (1, 3, 2):
            own_part(d, 0).wait_send()

        @pl.when(has_prev)
        def _():
            for j in range(4):
                deliver(j, y).wait_send()

        for d, core in ((1, 0), (1, 1), (3, 0), (3, 1), (2, 0), (2, 1), (0, 1)):
            share(d, core).wait_send()

    @pl.when(second)
    def _():
        for d in range(4):
            own_part(d, 1).wait_send()

        @pl.when(has_two)
        def _():
            for j in range(4):
                chain(j).wait_send()


def write_out(att, dq, dl, att_hbm, dq_hbm, dl_hbm, sem):
    copies = [pltpu.make_async_copy(dl, dl_hbm, sem.at[0])]
    for k in range(4):
        w = pl.ds(k * SLICE, SLICE)
        copies.append(pltpu.make_async_copy(att.at[w], att_hbm.at[w], sem.at[1 + k]))
        copies.append(pltpu.make_async_copy(dq.at[w], dq_hbm.at[w], sem.at[5 + k]))
    for cp in copies:
        cp.start()
    for cp in copies:
        cp.wait()


def pinned(value):
    return pltpu.with_memory_space_constraint(value, pltpu.HBM)


def body(query, latent, segment, d_out):
    hbm = pl.BlockSpec(memory_space=pltpu.HBM)
    vspec = pl.BlockSpec(memory_space=pltpu.VMEM)
    V = pltpu.VMEM
    outs = (((TOK, HEADS * LAT), bf16), ((TOK, HEADS * WIDTH), bf16), ((TOK, WIDTH), f32))
    made = pl.pallas_call(
        kernel,
        out_shape=tuple(V(s, t) for s, t in outs),
        in_specs=[hbm, hbm, hbm, hbm],
        out_specs=(vspec, vspec, vspec),
        scratch_shapes=[
            V((PAIRS, TOK, 2 * WIDTH), bf16),
            V((PAIRS, TOK, 2 * LAT), bf16),
            V((3 * TOK, PADW), bf16),
            V((3 * TOK, PADW), bf16),
            V((2, PADW, WIN), bf16),
            V((2, PADW, WIN), bf16),
            V((2, WIN, 1536), bf16),
            V((2, WIN, 1536), bf16),
            V((12, 256, WIN), bf16),
            V((12, 256, WIN), bf16),
            V((128, WIN), f32),
            V((64, WIN), f32),
            V((3, 1, TOK), jnp.int32),
            V((2, 3 * TOK, PADW), f32),
            V((3 * TOK, WIDTH), f32),
            V((TOK, WIDTH), bf16),
            V((TOK, WIDTH), bf16),
            V((TOK, WIDTH), bf16),
            V((4, SLICE, WIDTH), bf16),
            V((TOK, WIDTH), bf16),
            V((TOK, WIDTH), bf16),
            V((7, SLICE, WIDTH), bf16),
            V((TOK, WIDTH), bf16),
            V((TOK, WIDTH), bf16),
            V((12, 256, WIN // 2), f32),
            V((12, 256, WIN // 2), f32),
            pltpu.SemaphoreType.DMA((2, PAIRS + 1)),
            pltpu.SemaphoreType.DMA((34,)),
            pltpu.SemaphoreType.DMA((34,)),
        ],
        compiler_params=pltpu.CompilerParams(
            collective_id=0, has_side_effects=True, vmem_limit_bytes=50 << 20
        ),
    )(pinned(query), pinned(latent), pinned(segment.reshape(1, TOK)), pinned(d_out))
    return pl.pallas_call(
        write_out,
        out_shape=tuple(jax.ShapeDtypeStruct(s, t) for s, t in outs),
        in_specs=[pl.BlockSpec(memory_space=pl.ANY)] * 3,
        out_specs=(hbm, hbm, hbm),
        scratch_shapes=[pltpu.SemaphoreType.DMA((9,))],
        compiler_params=pltpu.CompilerParams(vmem_limit_bytes=1 << 20),
    )(*made)


def solution(mesh):
    in_specs = (P("ctx", "head"), P("ctx", None), P("ctx"), P("ctx", "head"))
    out_specs = (P("ctx", "head"), P("ctx", "head"), P("ctx", None))
    return jax.shard_map(body, mesh=mesh, in_specs=in_specs, out_specs=out_specs, check_vma=False)
```
